128 devices in a mesh: dom: 16 (over x, z), blk: 8 (over y, core).
Axes of the slice: x: 4, y: 4, z: 4, core: 2. Of those that a mesh axis runs over, the one named last changes fastest.
Arguments:
- multipliers: float32 [8, 96, 64, 256], P('blk', 'dom'), may hold values from -6 to 6
- residual: float32 [8, 96, 64, 256], P('blk', 'dom')
- dir_prev: float32 [8, 96, 64, 256], P('blk', 'dom'), may hold values from -6 to 6
- rho_prev: float32 [64], replicated, may hold values from 10 to 100
- face_ids: int32 [8, 32, 6], P('blk'), may hold values from 0 to 95, as said below
- face_sign: int32 [8, 32, 6], P('blk'), may hold values from -1 to 1, as said below
- dual_blocks: bfloat16 [8, 32, 1536, 1536], P('blk', 'dom'), as said below
- dirichlet_blocks: bfloat16 [8, 32, 1536, 1536], P('blk', 'dom'), as said below
- coupling: bfloat16 [8, 32, 256, 1536], P('blk', 'dom'), may hold values from -0.15625 to 0.15625
- corner_ids: int32 [8, 32, 256], P('blk', 'dom'), may hold values from 0 to 6143, as said below
- coarse_inv: bfloat16 [16, 8, 768, 768], P('dom', 'blk'), as said below
Outputs:
- new_multipliers: float32 [8, 96, 64, 256], P('blk', 'dom')
- new_residual: float32 [8, 96, 64, 256], P('blk', 'dom')
- direction: float32 [8, 96, 64, 256], P('blk', 'dom')
- rho_now: float32 [64], replicated
- reduction: float32 [64], replicated
The draws below stay inside these ranges and needn't reach their ends.
Inputs may be any that keep to these rules, and one draw needn't show every extreme that they name: `face_ids`: in each column b every face index below 96 is named by exactly two slots, of subdomains held by two different indices of dom; face f is owned by dom index f // 6. The 2 subdomains of one dom index name at most 2 faces of any one owner, and in every column some pairs of a dom index and an owner reach 2. `face_sign`: of the two slots that name one face, one has +1 and the other -1. `dual_blocks`: each block is symmetric positive definite. `dirichlet_blocks`: each block is symmetric positive definite. `coarse_inv`: each block is symmetric positive definite. `corner_ids`: the corners of one subdomain are distinct, and corner k lies in coarse block k // 32, that is, its index n satisfies n // 768 = k // 32.
All inputs are finite; a program needn't handle non-finite values.
Results may differ from the reference program's by a relative error of at most 0.033.
Values may be sent and summed in bfloat16 or wider, within the bound.
No kernel may reach another device: no remote copies, remote signals or barrier semaphores. Data moves between devices by JAX's collectives and lax.ppermute only.
A program may use at most 128 MiB of HBM per device.

```python
import math
import jax
import jax.numpy as jnp
from jax import lax

FDOF = 256
CASES = 64
FPS = 6
SUB_DEV = 2
CB = 768
NCD = 256
LOCAL = 1536
FACE_DEV = 6
CAP = 2
NSC = 32
NFC = 96
N_DOM = 16
N_BLK = 8


def face_pattern(key):
    base_key = jax.random.fold_in(key, 5)
    slot_total = FPS * SUB_DEV

    def shuffled(place_key_one):
        return jax.random.permutation(place_key_one, slot_total)

    def column_pattern(column_key):
        perm_key, place_key = jax.random.split(column_key)
        offsets_perm = jax.random.permutation(perm_key, N_DOM)
        element = jnp.arange(slot_total)
        cycle_index = 1 + jnp.maximum(element - CAP, 0) % (N_DOM - 1)
        offsets = jnp.where(element < CAP, offsets_perm[0], offsets_perm[cycle_index])
        dom_rows = jnp.arange(N_DOM)
        owner = (dom_rows[:, None] - offsets[None, :]) % N_DOM
        faces = owner * FACE_DEV + (element % FACE_DEV)[None, :]
        signs = jnp.broadcast_to(jnp.where(element < FACE_DEV, 1, -1)[None, :], (N_DOM, slot_total))
        place_keys = jax.random.split(place_key, N_DOM)
        placement = jax.vmap(shuffled)(place_keys)
        inverse = jnp.argsort(placement, axis=1, stable=True)
        faces = jnp.take_along_axis(faces, inverse, axis=1)
        signs = jnp.take_along_axis(signs, inverse, axis=1)
        return (faces.reshape(N_DOM * SUB_DEV, FPS).astype(jnp.int32), signs.reshape(N_DOM * SUB_DEV, FPS).astype(jnp.int32))
    column_keys = jax.random.split(base_key, N_BLK)
    return jax.vmap(column_pattern)(column_keys)


def draw_face_ids(key, part):
    return face_pattern(key)[0]


def draw_face_sign(key, part):
    return face_pattern(key)[1]


def draw_corner_ids(key, part):
    base_key = jax.random.fold_in(key, 31)
    share = NCD // N_BLK
    count = N_BLK * N_DOM * SUB_DEV * N_BLK
    keys = jax.random.split(base_key, count)

    def one_perm(perm_key):
        return jax.random.permutation(perm_key, CB)[:share]
    picks = jax.vmap(one_perm)(keys).reshape(N_BLK, N_DOM * SUB_DEV, N_BLK, share)
    sub_index = jnp.arange(N_DOM * SUB_DEV)[None, :, None, None]
    block_index = jnp.arange(N_BLK)[None, None, :, None]
    first = picks[:, :, :, :1]
    shift_high = jnp.where((sub_index == 0) & (block_index == N_BLK - 1), CB - 1 - first, 0)
    shift_low = jnp.where((sub_index == 0) & (block_index == 0), -first, 0)
    moved = (picks + shift_high + shift_low) % CB
    ids = moved + block_index * CB
    return ids.reshape(N_BLK, N_DOM * SUB_DEV, NCD).astype(jnp.int32)


def spd_stack(key, leading, matrix_order):
    block_count = leading[0] * leading[1]

    def single_block(block_index):
        block_key = jax.random.fold_in(key, block_index)
        noise_key, diag_key = jax.random.split(block_key)
        noise_vals = jax.random.normal(noise_key, (matrix_order, matrix_order), jnp.float32)
        symmetric = (noise_vals + noise_vals.T) * (0.7 / math.sqrt(2.0 * matrix_order))
        diagonal = jnp.exp(jax.random.uniform(diag_key, (matrix_order,), jnp.float32, math.log(2.2), math.log(4.4)))
        return (symmetric + jnp.diag(diagonal)).astype(jnp.bfloat16)
    blocks = lax.map(single_block, jnp.arange(block_count))
    return blocks.reshape(leading + (matrix_order, matrix_order))


def draw_dual_blocks(key, part):
    return spd_stack(jax.random.fold_in(key, 21), (N_BLK, N_DOM * SUB_DEV), FPS * FDOF)


def draw_dirichlet_blocks(key, part):
    return spd_stack(jax.random.fold_in(key, 22), (N_BLK, N_DOM * SUB_DEV), FPS * FDOF)


def draw_coarse_inv(key, part):
    return spd_stack(jax.random.fold_in(key, 23), (N_DOM, N_BLK), CB)


def draw_residual(key, part):
    noise_key = jax.random.fold_in(key, 11)
    shape = (N_BLK, N_DOM * FACE_DEV, CASES, FDOF)
    owner = (jnp.arange(N_DOM * FACE_DEV) // FACE_DEV).astype(jnp.float32)
    column = jnp.arange(N_BLK).astype(jnp.float32)
    rise = (1.0 + 2.0 * owner / (N_DOM - 1))[None, :, None, None] * (1.0 + 0.5 * column / max(N_BLK - 1, 1))[:, None, None, None]
    base_vals = jax.random.normal(noise_key, shape, jnp.float32)
    return (base_vals * rise).astype(jnp.float32)


def steps_of(rng, extent, shards, least, high):
    gain, own = 1.0, jax.random.fold_in(rng, 6)
    for position, parts in shards:
        steps = jnp.exp(jax.random.uniform(jax.random.fold_in(own, position), (parts,), jnp.float32, least / len(shards), high / len(shards)))
        gain = gain * jnp.repeat(steps, extent[position] // parts).reshape([-1 if axis == position else 1 for axis in range(len(extent))])
    return gain


def noise(stream_key, extent, scale, most, cuts=(), held_as=jnp.bfloat16):
    result = jax.random.normal(stream_key, extent, jnp.float32) * scale
    if len(cuts) > 0:
        result = steps_of(stream_key, extent, cuts, -0.22, 0.18) * result
    return jnp.clip(result, min=-most, max=most).astype(held_as)


def setup_inputs(seed: int = 0) -> dict:
    key_list = jax.random.split(jax.random.key(seed), 12)
    return {
        "multipliers": noise(key_list[0], (N_BLK, NFC, CASES, FDOF), 1.0, 6.0, ((0, 8), (1, 16)), jnp.float32),
        "residual": draw_residual(jax.random.fold_in(key_list[11], 71), 0),
        "dir_prev": noise(key_list[2], (N_BLK, NFC, CASES, FDOF), 1.0, 6.0, ((0, 8), (1, 16)), jnp.float32),
        "rho_prev": jnp.clip(jnp.exp(jax.random.uniform(key_list[3], (CASES,), jnp.float32, math.log(10.0), math.log(100.0))), 10.0, 100.0),
        "face_ids": draw_face_ids(jax.random.fold_in(key_list[11], 71), 0),
        "face_sign": draw_face_sign(jax.random.fold_in(key_list[11], 71), 0),
        "dual_blocks": draw_dual_blocks(jax.random.fold_in(key_list[11], 71), 0),
        "dirichlet_blocks": draw_dirichlet_blocks(jax.random.fold_in(key_list[11], 71), 0),
        "coupling": noise(key_list[8], (N_BLK, NSC, NCD, LOCAL), LOCAL ** -0.5, 0.15625, ((0, 8), (1, 16))),
        "corner_ids": draw_corner_ids(jax.random.fold_in(key_list[11], 71), 0),
        "coarse_inv": draw_coarse_inv(jax.random.fold_in(key_list[11], 71), 0),
    }


def pull_slots(vector, face_ids, face_sign):
    vector_half = vector.astype(jnp.bfloat16)

    def column_pick(column_vec, column_ids):
        return column_vec[column_ids]

    picked = jax.vmap(column_pick)(vector_half, face_ids)
    return picked * face_sign.astype(jnp.bfloat16)[:, :, :, None, None]


def local_products(slots, matrices):
    def column_product(operands):
        pieces, blocks = operands
        wide = blocks.astype(jnp.float32).reshape(N_DOM * SUB_DEV, FPS, FDOF, FPS * FDOF)
        return jnp.einsum("stcx,stxm->scm", pieces.astype(jnp.float32), wide)

    return lax.map(column_product, (slots, matrices))


def push_faces(totals, face_ids, face_sign):
    per_slot = totals.reshape(N_BLK, N_DOM * SUB_DEV, CASES, FPS, FDOF)
    per_slot = per_slot * face_sign.astype(jnp.float32)[:, :, None, :, None]
    rounded = lax.optimization_barrier(per_slot.astype(jnp.bfloat16)).astype(jnp.float32)
    rounded = jnp.transpose(rounded, (0, 1, 3, 2, 4)).reshape(N_BLK, N_DOM * SUB_DEV * FPS, CASES, FDOF)

    def column_add(column_ids, column_vals):
        start_sums = jnp.zeros((N_DOM * FACE_DEV, CASES, FDOF), jnp.float32)
        return start_sums.at[column_ids.reshape(-1)].add(column_vals)

    return jax.vmap(column_add)(face_ids, rounded)


def coarse_term(slots, coupling, corner_ids, coarse_inv):
    wide = coupling.astype(jnp.float32).reshape(N_BLK, N_DOM * SUB_DEV, NCD, FPS, FDOF)
    corner_terms = jnp.einsum("bjtcx,bjktx->bjck", slots.astype(jnp.float32), wide)
    corner_terms = corner_terms.reshape(N_BLK, N_DOM, SUB_DEV, CASES, NCD)
    index_rows = corner_ids.reshape(N_BLK, N_DOM, SUB_DEV, NCD)

    def column_assemble(column_terms, column_index):
        values = jnp.transpose(column_terms, (2, 0, 1, 3)).reshape(CASES, N_BLK * SUB_DEV * NCD)
        start_sums = jnp.zeros((CASES, N_BLK * CB), jnp.float32)
        return start_sums.at[:, column_index.reshape(-1)].add(values)

    coarse_rhs = jax.vmap(column_assemble, in_axes=(1, 1))(corner_terms, index_rows)
    coarse_half = lax.optimization_barrier(coarse_rhs.astype(jnp.bfloat16))
    coarse_half = coarse_half.astype(jnp.float32).reshape(N_DOM, CASES, N_BLK, CB)
    solved = jnp.einsum("dcbm,dbmn->dcbn", coarse_half, coarse_inv.astype(jnp.float32))
    solved = lax.optimization_barrier(solved.astype(jnp.bfloat16))
    solved = solved.astype(jnp.float32).reshape(N_DOM, CASES, N_BLK * CB)

    def column_pick(column_sol, column_index):
        return column_sol[:, column_index]

    picked = jax.vmap(column_pick, in_axes=(0, 1))(solved, index_rows)
    picked = jnp.transpose(picked, (2, 0, 3, 1, 4)).reshape(N_BLK, N_DOM * SUB_DEV, CASES, NCD)
    return jnp.einsum("bjck,bjkl->bjcl", picked, coupling.astype(jnp.float32))


def reference(multipliers, residual, dir_prev, rho_prev, face_ids, face_sign, dual_blocks, dirichlet_blocks, coupling, corner_ids, coarse_inv):
    total_count = N_BLK * N_DOM * FACE_DEV * FDOF
    slots = pull_slots(residual, face_ids, face_sign)
    precond_res = push_faces(local_products(slots, dirichlet_blocks), face_ids, face_sign)
    rho_now = jnp.sum(residual * precond_res, axis=(0, 1, 3)) / total_count
    res_mean = jnp.sum(residual * residual, axis=(0, 1, 3)) / total_count
    beta_ratio = rho_now / rho_prev
    direction = precond_res + beta_ratio[None, None, :, None] * dir_prev
    slots = pull_slots(direction, face_ids, face_sign)
    totals = local_products(slots, dual_blocks) + coarse_term(slots, coupling, corner_ids, coarse_inv)
    image = push_faces(totals, face_ids, face_sign)
    curvature = jnp.sum(direction * image, axis=(0, 1, 3)) / total_count
    alpha_step = rho_now / curvature
    new_multipliers = multipliers + alpha_step[None, None, :, None] * direction
    new_residual = residual - alpha_step[None, None, :, None] * image
    reduction = (jnp.sum(new_residual * new_residual, axis=(0, 1, 3)) / total_count) / res_mean
    return new_multipliers, new_residual, direction, rho_now, reduction
```

```python
import functools

import jax
import jax.numpy as jnp
from jax import lax
from jax.experimental import pallas as pl
from jax.experimental.pallas import tpu as pltpu
from jax.sharding import Mesh
from jax.sharding import PartitionSpec as P

DOM = ("dom_0", "dom_1")
BLK = ("blk_0", "blk_1")

F32 = jnp.float32
BF16 = jnp.bfloat16

FACES = 6
SLOTS = 12
N_DOM = 16
N_BLK = 8
COL_FACES = FACES * N_DOM
COL_SLOTS = SLOTS * N_DOM
CASES = 64
FDOF = 256
LOCAL = 1536
NCD = 256
CB = 768
TOTAL = float(N_BLK * COL_FACES * FDOF)


VMEM_SPEC = pl.BlockSpec(memory_space=pltpu.VMEM)
SMEM_SPEC = pl.BlockSpec(memory_space=pltpu.SMEM)


def whole(shape):
    return pl.BlockSpec(shape, lambda *_: (0,) * len(shape))


def params(mib=32):
    return pltpu.CompilerParams(vmem_limit_bytes=mib * 1024 * 1024)


def shape_of(shape, dtype):
    return jax.ShapeDtypeStruct(shape, dtype)


def pair(a, b):
    return jnp.concatenate([a, b], axis=0)


def split_two(tile):
    high = tile.astype(BF16).astype(F32)
    return high, tile - high


def pack_kernel(res_ref, dir_ref, out_ref):
    for kind, ref in enumerate((res_ref, dir_ref)):
        for g in range(8):
            for h in range(2):
                for q in range(FACES // 2):
                    rows, lanes = pl.ds(8 * g, 8), pl.ds(128 * h, 128)
                    tile = pair(ref[2 * q, rows, lanes], ref[2 * q + 1, rows, lanes])
                    out_ref[2 * g + h, pl.ds(kind * 48 + 16 * q, 16), :] = tile.astype(BF16)


def pack(res, dirp):
    return pl.pallas_call(
        pack_kernel,
        out_shape=shape_of((N_DOM, 96, 128), BF16),
        in_specs=[VMEM_SPEC, VMEM_SPEC],
        out_specs=VMEM_SPEC,
        compiler_params=params(),
        name="pack",
    )(res, dirp)


def faces_wide(msg_ref, first, wide_ref):
    for o in range(N_DOM):
        for q in range(FACES // 2):
            tile = msg_ref[o, pl.ds(first + 16 * q, 16), :].astype(F32)
            wide_ref[FACES * o + 2 * q] = tile[:8]
            wide_ref[FACES * o + 2 * q + 1] = tile[8:]


def emit_slots(wide_ref, ids_ref, sign_ref, out_ref):
    for j in range(N_DOM):
        for q in range(SLOTS // 2):
            e = SLOTS * j + 2 * q
            tile = pair(
                wide_ref[ids_ref[e]] * sign_ref[e],
                wide_ref[ids_ref[e + 1]] * sign_ref[e + 1],
            )
            out_ref[j, pl.ds(16 * q, 16), :] = tile.astype(BF16)


def scatter_slots(msg_ref, place_ref, both_ref):
    for j in range(N_DOM):
        for q in range(SLOTS // 2):
            e = SLOTS * j + 2 * q
            tile = msg_ref[j, pl.ds(16 * q, 16), :].astype(F32)
            both_ref[place_ref[e]] = tile[:8]
            both_ref[place_ref[e + 1]] = tile[8:]


def pull_kernel(ids_ref, sign_ref, msg_ref, out_ref, wide_ref):
    faces_wide(msg_ref, 0, wide_ref)
    emit_slots(wide_ref, ids_ref, sign_ref, out_ref)


def pull(ids, sign, msg):
    return pl.pallas_call(
        pull_kernel,
        out_shape=shape_of((N_DOM, 96, 128), BF16),
        in_specs=[SMEM_SPEC, SMEM_SPEC, VMEM_SPEC],
        out_specs=VMEM_SPEC,
        scratch_shapes=[pltpu.VMEM((COL_FACES, 8, 128), F32)],
        compiler_params=params(),
        name="pull",
    )(ids, sign, msg)


def unpack_slots(msg_ref, x_ref):
    for m in range(4):
        for h in range(2):
            for q6 in range(6):
                s, q = divmod(q6, 3)
                upper = msg_ref[4 * m + h, pl.ds(16 * q6, 16), :].astype(F32)
                lower = msg_ref[4 * m + 2 + h, pl.ds(16 * q6, 16), :].astype(F32)
                rows = pl.ds(16 * m, 16)
                x_ref[s, rows, pl.ds(512 * q + 128 * h, 128)] = pair(upper[:8], lower[:8]).astype(BF16)
                x_ref[s, rows, pl.ds(512 * q + 256 + 128 * h, 128)] = pair(upper[8:], lower[8:]).astype(BF16)


def send_rows(y, s, q, sign_ref, out_ref):
    first = sign_ref[6 * s + 2 * q]
    second = sign_ref[6 * s + 2 * q + 1]
    start = pl.multiple_of((3 * s + q) * 16, 16)
    for g in range(8):
        for h in range(2):
            tile = pair(
                y[8 * g : 8 * g + 8, 128 * h : 128 * h + 128] * first,
                y[8 * g : 8 * g + 8, 256 + 128 * h : 384 + 128 * h] * second,
            )
            out_ref[2 * g + h, pl.ds(start, 16), :] = tile.astype(BF16)


def lane_tiles(v):
    return sum(v[:, 128 * k : 128 * k + 128] for k in range(4))


def send_sums(acc, out_ref):
    high, low = split_two(acc)
    for g in range(8):
        tile = pair(high[8 * g : 8 * g + 8], low[8 * g : 8 * g + 8]).astype(BF16)
        for h in range(2):
            out_ref[2 * g + h, pl.ds(96, 16), :] = tile


def precond_kernel(sign_ref, msg_ref, mat_ref, out_ref, x_ref, acc_ref):
    s, q = pl.program_id(0), pl.program_id(1)

    @pl.when((s == 0) & (q == 0))
    def _():
        unpack_slots(msg_ref, x_ref)
        acc_ref[...] = jnp.zeros_like(acc_ref)

    y = jnp.dot(x_ref[s], mat_ref[0], preferred_element_type=F32)
    x = x_ref[s, :, pl.ds(pl.multiple_of(512 * q, 512), 512)].astype(F32)
    acc_ref[...] += lane_tiles(x * y)
    send_rows(y, s, q, sign_ref, out_ref)

    @pl.when((s == 1) & (q == 2))
    def _():
        send_sums(acc_ref[...], out_ref)


def precond(sign, msg, mats):
    return pl.pallas_call(
        precond_kernel,
        grid=(2, 3),
        out_shape=shape_of((N_DOM, 112, 128), BF16),
        in_specs=[
            SMEM_SPEC,
            whole((N_DOM, 96, 128)),
            pl.BlockSpec((1, LOCAL, 512), lambda s, q: (s, 0, q)),
        ],
        out_specs=whole((N_DOM, 112, 128)),
        scratch_shapes=[pltpu.VMEM((2, CASES, LOCAL), BF16), pltpu.VMEM((CASES, 128), F32)],
        compiler_params=params(),
        name="precond",
    )(sign, msg, mats)


def rho_kernel(msg_ref, out_ref):
    total = jnp.zeros((16, 128), F32)
    for j in range(N_DOM):
        total += msg_ref[j].astype(F32)
    tile = total[:8] + total[8:]
    for b in range(N_BLK):
        out_ref[b] = tile


def rho_parts(msg):
    return pl.pallas_call(
        rho_kernel,
        grid=(1,),
        out_shape=shape_of((N_BLK, 8, 128), F32),
        in_specs=[pl.BlockSpec((N_DOM, 16, 128), lambda i: (0, 6, 0))],
        out_specs=whole((N_BLK, 8, 128)),
        compiler_params=params(),
        name="rho_parts",
    )(msg)


def faces_kernel(place_ref, msg_ref, out_ref, both_ref):
    scatter_slots(msg_ref, place_ref, both_ref)
    out_ref[...] = both_ref[:COL_FACES] + both_ref[COL_FACES:]


def face_sums(place, msg):
    return pl.pallas_call(
        faces_kernel,
        out_shape=shape_of((COL_FACES, 8, 128), F32),
        in_specs=[SMEM_SPEC, VMEM_SPEC],
        out_specs=VMEM_SPEC,
        scratch_shapes=[pltpu.VMEM((COL_SLOTS, 8, 128), F32)],
        compiler_params=params(),
        name="face_sums",
    )(place, msg)


def all_of(parts_ref):
    return sum(parts_ref[b] for b in range(N_BLK))


def direction_kernel(ids_ref, sign_ref, parts_ref, prev_ref, p_ref, msg_ref, out_ref, rho_ref, wide_ref):
    rho = jnp.sum(all_of(parts_ref), axis=1, keepdims=True) * (1.0 / TOTAL)
    rho_ref[...] = jnp.broadcast_to(rho, (8, 128))
    beta = jnp.broadcast_to(rho / prev_ref[:, :1], (8, 128))
    faces_wide(msg_ref, 48, wide_ref)
    wide_ref[...] = p_ref[...] + beta[None] * wide_ref[...]
    emit_slots(wide_ref, ids_ref, sign_ref, out_ref)


def directions(ids, sign, parts, prev, p, msg):
    return pl.pallas_call(
        direction_kernel,
        out_shape=(shape_of((N_DOM, 96, 128), BF16), shape_of((8, 128), F32)),
        in_specs=[SMEM_SPEC, SMEM_SPEC] + [VMEM_SPEC] * 4,
        out_specs=(VMEM_SPEC, VMEM_SPEC),
        scratch_shapes=[pltpu.VMEM((COL_FACES, 8, 128), F32)],
        compiler_params=params(),
        name="directions",
    )(ids, sign, parts, prev, p, msg)


def corner_kernel(msg_ref, coupling_ref, x_ref, out_ref):
    unpack_slots(msg_ref, x_ref)
    for s in range(2):
        terms = lax.dot_general(
            coupling_ref[s], x_ref[s], (((1,), (1,)), ((), ())), preferred_element_type=F32
        )
        out_ref[:, pl.ds(64 * s, 64)] = terms.astype(BF16)


def corners(msg, coupling):
    return pl.pallas_call(
        corner_kernel,
        out_shape=(shape_of((2, CASES, LOCAL), BF16), shape_of((NCD, 128), BF16)),
        in_specs=[VMEM_SPEC, VMEM_SPEC],
        out_specs=(VMEM_SPEC, VMEM_SPEC),
        compiler_params=params(),
        name="corners",
    )(msg, coupling)


def dual_kernel(x_ref, mat_ref, out_ref):
    out_ref[0] = jnp.dot(x_ref[0], mat_ref[0], preferred_element_type=F32)


def dual(x, mats):
    return pl.pallas_call(
        dual_kernel,
        grid=(2, 3),
        out_shape=shape_of((2, CASES, LOCAL), F32),
        in_specs=[
            pl.BlockSpec((1, CASES, LOCAL), lambda s, q: (s, 0, 0)),
            pl.BlockSpec((1, LOCAL, 512), lambda s, q: (s, 0, q)),
        ],
        out_specs=pl.BlockSpec((1, CASES, 512), lambda s, q: (s, 0, q)),
        compiler_params=params(),
        cost_estimate=pl.CostEstimate(
            flops=4 * CASES * LOCAL * LOCAL, bytes_accessed=4 * LOCAL * LOCAL, transcendentals=0
        ),
        name="dual",
    )(x, mats)


def image_kernel(sign_ref, y_sign_ref, k_ref, p0, p1, p2, p3, x_ref, dual_ref, coupling_ref, out_ref, all_ref, pick_ref):
    my_y = y_sign_ref[0]
    for step, piece in enumerate((p0, p1, p2, p3)):
        chip = lax.rem(my_y + (4 - step), 4)
        for core in range(2):
            all_ref[2 * chip + core] = piece[core]
    for b in range(N_BLK):
        rows = all_ref[:, pl.ds(32 * b, 32), :].reshape(N_BLK * 32, 128)
        got = lax.dot_general(k_ref[b], rows, (((1,), (0,)), ((), ())), preferred_element_type=F32)
        summed = got[:64, :64] + got[64:, 64:]
        for s in range(2):
            pick_ref[s, pl.ds(32 * b, 32), :] = summed[32 * s : 32 * s + 32].astype(BF16)
    acc = jnp.zeros((CASES, 128), F32)
    for s in range(2):
        coarse = lax.dot_general(
            pick_ref[s], coupling_ref[s], (((0,), (0,)), ((), ())), preferred_element_type=F32
        )
        for q in range(3):
            lanes = slice(512 * q, 512 * q + 512)
            y = dual_ref[s, :, lanes] + coarse[:, lanes]
            acc += lane_tiles(x_ref[s, :, lanes].astype(F32) * y)
            send_rows(y, s, q, sign_ref, out_ref)
    send_sums(acc, out_ref)


def image_rows(sign, my_y, k_mat, pieces, x, dual_y, coupling):
    return pl.pallas_call(
        image_kernel,
        out_shape=shape_of((N_DOM, 112, 128), BF16),
        in_specs=[SMEM_SPEC, SMEM_SPEC] + [VMEM_SPEC] * 8,
        out_specs=VMEM_SPEC,
        scratch_shapes=[pltpu.VMEM((N_BLK, NCD, 128), BF16), pltpu.VMEM((2, NCD, CASES), BF16)],
        compiler_params=params(),
        name="image_rows",
    )(sign, my_y, k_mat, *pieces, x, dual_y, coupling)


def back_kernel(place_ref, at_ref, msg_ref, p_ref, first_ref, rho_ref, out_ref, both_ref):
    scatter_slots(msg_ref, place_ref, both_ref)
    total = jnp.zeros((16, 128), F32)
    for j in range(N_DOM):
        total += msg_ref[j, pl.ds(96, 16), :].astype(F32)
    s0 = jnp.zeros((8, 128), F32)
    s1 = jnp.zeros((8, 128), F32)
    s2 = jnp.zeros((8, 128), F32)
    for o in range(N_DOM):
        for q in range(FACES // 2):
            f = FACES * o + 2 * q
            one = both_ref[f] + both_ref[COL_FACES + f]
            two = both_ref[f + 1] + both_ref[COL_FACES + f + 1]
            res = first_ref[o, pl.ds(16 * q, 16), :].astype(F32)
            s0 += res[:8] * res[:8] + res[8:] * res[8:]
            s1 += res[:8] * one + res[8:] * two
            s2 += one * one + two * two
            out_ref[o, pl.ds(16 * q, 16), :] = pair(one, two).astype(BF16)
            out_ref[o, pl.ds(48 + 16 * q, 16), :] = pair(p_ref[f], p_ref[f + 1]).astype(BF16)
    base = at_ref[0]
    half = (1 - at_ref[1]).astype(F32)
    lane = lax.broadcasted_iota(jnp.int32, (8, 128), 1)
    stats = jnp.zeros((8, 128), F32)
    sums = (
        rho_ref[:, :1] * (half * (1.0 / N_BLK)),
        jnp.sum(total[:8] + total[8:], axis=1, keepdims=True) * half,
        jnp.sum(s0, axis=1, keepdims=True),
        jnp.sum(s1, axis=1, keepdims=True),
        jnp.sum(s2, axis=1, keepdims=True),
    )
    for k, value in enumerate(sums):
        value = jnp.broadcast_to(value, (8, 128))
        high, rest = split_two(value)
        stats = jnp.where(lane == base + k, high, stats)
        stats = jnp.where(lane == base + 64 + k, rest, stats)
    high, rest = split_two(stats)
    tile = pair(high, rest).astype(BF16)
    for o in range(N_DOM):
        out_ref[o, pl.ds(96, 16), :] = tile


def back(place, at, msg, p, first, rho):
    return pl.pallas_call(
        back_kernel,
        out_shape=shape_of((N_DOM, 112, 128), BF16),
        in_specs=[SMEM_SPEC, SMEM_SPEC] + [VMEM_SPEC] * 4,
        out_specs=VMEM_SPEC,
        scratch_shapes=[pltpu.VMEM((COL_SLOTS, 8, 128), F32)],
        compiler_params=params(),
        name="back",
    )(place, at, msg, p, first, rho)


def sums_parts(msg):
    return pl.pallas_call(
        rho_kernel,
        grid=(1,),
        out_shape=shape_of((N_BLK, 8, 128), F32),
        in_specs=[pl.BlockSpec((N_DOM, 16, 128), lambda i: (0, 6, 0))],
        out_specs=whole((N_BLK, 8, 128)),
        compiler_params=params(),
        name="sums_parts",
    )(msg)


def final_kernel(parts_ref, prev_ref, msg_ref, lam_ref, res_ref, dir_ref, lam_out, res_out, dir_out, rho_out, red_out):
    both = all_of(parts_ref)
    total = both[:, :64] + both[:, 64:]
    for g in range(8):
        rho = total[:, 8 * g : 8 * g + 1]
        curve = total[:, 8 * g + 1 : 8 * g + 2] * (1.0 / TOTAL)
        s0 = total[:, 8 * g + 2 : 8 * g + 3]
        s1 = total[:, 8 * g + 3 : 8 * g + 4]
        s2 = total[:, 8 * g + 4 : 8 * g + 5]
        alpha = rho / curve
        rows = pl.ds(8 * g, 8)
        beta = rho / prev_ref[rows, :]
        rho_out[rows, :] = rho
        red_out[rows, :] = (s0 - alpha * (2.0 * s1 - alpha * s2)) / s0
        alpha = jnp.broadcast_to(alpha, (8, 128))
        beta = jnp.broadcast_to(beta, (8, 128))
        for h in range(2):
            lanes = pl.ds(128 * h, 128)
            for q in range(FACES // 2):
                image = msg_ref[2 * g + h, pl.ds(16 * q, 16), :].astype(F32)
                p = msg_ref[2 * g + h, pl.ds(48 + 16 * q, 16), :].astype(F32)
                for k in range(2):
                    f = 2 * q + k
                    half = slice(8 * k, 8 * k + 8)
                    direction = p[half] + beta * dir_ref[f, rows, lanes]
                    dir_out[f, rows, lanes] = direction
                    lam_out[f, rows, lanes] = lam_ref[f, rows, lanes] + alpha * direction
                    res_out[f, rows, lanes] = res_ref[f, rows, lanes] - alpha * image[half]


def final(parts, prev, msg, lam, res, dirp):
    field = shape_of((FACES, CASES, FDOF), F32)
    column = shape_of((CASES, 1), F32)
    return pl.pallas_call(
        final_kernel,
        out_shape=(field, field, field, column, column),
        in_specs=[VMEM_SPEC] * 6,
        out_specs=(VMEM_SPEC,) * 5,
        compiler_params=params(),
        name="final",
    )(parts, prev, msg, lam, res, dirp)


def exchange(value, axis):
    return lax.all_to_all(value, axis, 0, 0, tiled=True)


def coarse_matrix(corner_ids, coarse_inv):
    me = lax.axis_index(BLK)
    ids = lax.all_gather(corner_ids, BLK, axis=0)
    ids = ids.reshape(N_BLK, 2, N_BLK, 32)
    ids = lax.dynamic_index_in_dim(ids, me, 2, keepdims=False) - me * CB
    spot = jnp.arange(CB)
    mine = (ids.reshape(-1)[:, None] == spot[None]).astype(BF16)
    other = (jnp.swapaxes(ids, 0, 1).reshape(-1)[None] == spot[:, None]).astype(BF16)
    half = jnp.dot(mine, coarse_inv, preferred_element_type=F32).astype(BF16)
    full = jnp.dot(half, other, preferred_element_type=F32).astype(BF16)
    every = lax.all_gather(full, BLK, axis=0)
    own = lax.dynamic_slice_in_dim(every, 64 * me, 64, 1)
    return jnp.concatenate([own[:, :, :256], own[:, :, 256:]], axis=1)


def on_device(
    multipliers,
    residual,
    dir_prev,
    rho_prev,
    face_ids,
    face_sign,
    dual_blocks,
    dirichlet_blocks,
    coupling,
    corner_ids,
    coarse_inv,
):
    me = lax.axis_index(DOM)
    case_group = me // 2
    ids = face_ids[0].reshape(-1)
    sign_int = face_sign[0].reshape(-1)
    sign = sign_int.astype(F32)
    place = jnp.where(sign_int < 0, ids + COL_FACES, ids)
    my_sign = lax.dynamic_slice_in_dim(sign, me * SLOTS, SLOTS)
    at = jnp.stack([8 * case_group, me % 2]).astype(jnp.int32)
    my_y = lax.axis_index("blk_0").astype(jnp.int32)[None]
    prev = rho_prev[:, None]
    prev_mine = jnp.broadcast_to(lax.dynamic_slice_in_dim(prev, 8 * case_group, 8), (8, 128))

    first = exchange(pack(residual[0], dir_prev[0]), DOM)
    slots = exchange(pull(ids, sign, first), DOM)
    rows = exchange(precond(my_sign, slots, dirichlet_blocks[0]), DOM)
    parts = exchange(rho_parts(rows), BLK)
    p = face_sums(place, rows)
    out_slots, rho = directions(ids, sign, parts, prev_mine, p, first)
    dir_slots = exchange(out_slots, DOM)
    x, terms = corners(dir_slots, coupling[0])
    other = lax.ppermute(terms, "blk_1", [(0, 1), (1, 0)])
    core = lax.axis_index("blk_1")
    chip = jnp.stack([jnp.where(core == 0, terms, other), jnp.where(core == 0, other, terms)])
    pieces = [chip] + [
        lax.ppermute(chip, "blk_0", [(i, (i + k) % 4) for i in range(4)]) for k in range(1, 4)
    ]
    dual_y = dual(x, dual_blocks[0])
    k_mat = coarse_matrix(corner_ids[0], coarse_inv[0, 0])
    image = exchange(image_rows(my_sign, my_y, k_mat, pieces, x, dual_y, coupling[0]), DOM)
    msg = exchange(back(place, at, image, p, first, rho), DOM)
    sums = exchange(sums_parts(msg), BLK)
    lam, res, direction, rho_now, reduction = final(
        sums, prev, msg, multipliers[0], residual[0], dir_prev[0]
    )
    return (lam[None], res[None], direction[None], rho_now[:, 0], reduction[:, 0])


def solution(mesh):
    split = Mesh(mesh.devices.reshape(4, 4, 4, 2), ("dom_0", "dom_1", "blk_0", "blk_1"))
    in_specs = (
        P(BLK, DOM, None, None),
        P(BLK, DOM, None, None),
        P(BLK, DOM, None, None),
        P(),
        P(BLK, None, None),
        P(BLK, None, None),
        P(BLK, DOM, None, None),
        P(BLK, DOM, None, None),
        P(BLK, DOM, None, None),
        P(BLK, DOM, None),
        P(DOM, BLK, None, None),
    )
    out_specs = (
        P(BLK, DOM, None, None),
        P(BLK, DOM, None, None),
        P(BLK, DOM, None, None),
        P(),
        P(),
    )
    return jax.shard_map(
        on_device, mesh=split, in_specs=in_specs, out_specs=out_specs, check_vma=False
    )
```

```python
import functools

import jax
import jax.numpy as jnp
from jax import lax
from jax.experimental import pallas as pl
from jax.experimental.pallas import tpu as pltpu
from jax.sharding import Mesh
from jax.sharding import PartitionSpec as P

DOM = ("dom_0", "dom_1")
BLK = ("blk_0", "blk_1")

F32 = jnp.float32
BF16 = jnp.bfloat16

FACES = 6
SLOTS = 12
N_DOM = 16
N_BLK = 8
COL_FACES = FACES * N_DOM
COL_SLOTS = SLOTS * N_DOM
CASES = 64
FDOF = 256
LOCAL = 1536
NCD = 256
CB = 768
TOTAL = float(N_BLK * COL_FACES * FDOF)


VMEM_SPEC = pl.BlockSpec(memory_space=pltpu.VMEM)
SMEM_SPEC = pl.BlockSpec(memory_space=pltpu.SMEM)
HBM_SPEC = pl.BlockSpec(memory_space=pl.ANY)


def whole(shape):
    return pl.BlockSpec(shape, lambda *_: (0,) * len(shape))


def params(mib=16):
    return pltpu.CompilerParams(vmem_limit_bytes=mib * 1024 * 1024)


def shape_of(shape, dtype):
    return jax.ShapeDtypeStruct(shape, dtype)


def pair(a, b):
    return jnp.concatenate([a, b], axis=0)


def split_two(tile):
    high = tile.astype(BF16).astype(F32)
    return high, tile - high


def pack_kernel(res_hbm, dir_hbm, out_ref, field_ref, sems):
    copies = []
    for kind, hbm in enumerate((res_hbm, dir_hbm)):
        for q in range(FACES // 2):
            copy = pltpu.make_async_copy(
                hbm.at[pl.ds(2 * q, 2)], field_ref.at[kind, pl.ds(2 * q, 2)], sems.at[kind, q]
            )
            copy.start()
            copies.append((kind, q, copy))
    for kind, q, copy in copies:
        copy.wait()
        for g in range(8):
            for h in range(2):
                rows, lanes = pl.ds(8 * g, 8), pl.ds(128 * h, 128)
                tile = pair(field_ref[kind, 2 * q, rows, lanes], field_ref[kind, 2 * q + 1, rows, lanes])
                out_ref[2 * g + h, pl.ds(kind * 48 + 16 * q, 16), :] = tile.astype(BF16)


def pack(res, dirp):
    return pl.pallas_call(
        pack_kernel,
        out_shape=shape_of((N_DOM, 96, 128), BF16),
        in_specs=[HBM_SPEC, HBM_SPEC],
        out_specs=VMEM_SPEC,
        scratch_shapes=[
            pltpu.VMEM((2, FACES, CASES, FDOF), F32),
            pltpu.SemaphoreType.DMA((2, FACES // 2)),
        ],
        compiler_params=params(58),
        name="pack",
    )(res, dirp)


def faces_wide(msg_ref, first, wide_ref):
    for o in range(N_DOM):
        for q in range(FACES // 2):
            tile = msg_ref[o, pl.ds(first + 16 * q, 16), :].astype(F32)
            wide_ref[FACES * o + 2 * q] = tile[:8]
            wide_ref[FACES * o + 2 * q + 1] = tile[8:]


def emit_slots(wide_ref, ids_ref, sign_ref, out_ref):
    for j in range(N_DOM):
        for q in range(SLOTS // 2):
            e = SLOTS * j + 2 * q
            tile = pair(
                wide_ref[ids_ref[e]] * sign_ref[e],
                wide_ref[ids_ref[e + 1]] * sign_ref[e + 1],
            )
            out_ref[j, pl.ds(16 * q, 16), :] = tile.astype(BF16)


def scatter_slots(msg_ref, place_ref, both_ref):
    for j in range(N_DOM):
        for q in range(SLOTS // 2):
            e = SLOTS * j + 2 * q
            tile = msg_ref[j, pl.ds(16 * q, 16), :].astype(F32)
            both_ref[place_ref[e]] = tile[:8]
            both_ref[place_ref[e + 1]] = tile[8:]


def pull_kernel(ids_ref, sign_ref, msg_ref, out_ref, wide_ref):
    faces_wide(msg_ref, 0, wide_ref)
    emit_slots(wide_ref, ids_ref, sign_ref, out_ref)


def pull(ids, sign, msg):
    return pl.pallas_call(
        pull_kernel,
        out_shape=shape_of((N_DOM, 96, 128), BF16),
        in_specs=[SMEM_SPEC, SMEM_SPEC, VMEM_SPEC],
        out_specs=VMEM_SPEC,
        scratch_shapes=[pltpu.VMEM((COL_FACES, 8, 128), F32)],
        compiler_params=params(),
        name="pull",
    )(ids, sign, msg)


def unpack_slots(msg_ref, x_ref):
    for m in range(4):
        for h in range(2):
            for q6 in range(6):
                s, q = divmod(q6, 3)
                upper = msg_ref[4 * m + h, pl.ds(16 * q6, 16), :].astype(F32)
                lower = msg_ref[4 * m + 2 + h, pl.ds(16 * q6, 16), :].astype(F32)
                rows = pl.ds(16 * m, 16)
                x_ref[s, rows, pl.ds(512 * q + 128 * h, 128)] = pair(upper[:8], lower[:8]).astype(BF16)
                x_ref[s, rows, pl.ds(512 * q + 256 + 128 * h, 128)] = pair(upper[8:], lower[8:]).astype(BF16)


def send_rows(y, s, q, sign_ref, out_ref):
    first = sign_ref[6 * s + 2 * q]
    second = sign_ref[6 * s + 2 * q + 1]
    start = (3 * s + q) * 16
    for g in range(8):
        for h in range(2):
            tile = pair(
                y[8 * g : 8 * g + 8, 128 * h : 128 * h + 128] * first,
                y[8 * g : 8 * g + 8, 256 + 128 * h : 384 + 128 * h] * second,
            )
            out_ref[2 * g + h, pl.ds(start, 16), :] = tile.astype(BF16)


def lane_tiles(v):
    return sum(v[:, 128 * k : 128 * k + 128] for k in range(4))


def send_sums(acc, out_ref):
    high, low = split_two(acc)
    for g in range(8):
        tile = pair(high[8 * g : 8 * g + 8], low[8 * g : 8 * g + 8]).astype(BF16)
        for h in range(2):
            out_ref[2 * g + h, pl.ds(96, 16), :] = tile


def load_columns(mat_hbm, s, mat_ref, sems):
    copies = []
    for q in range(3):
        lanes = pl.ds(512 * q, 512)
        copy = pltpu.make_async_copy(mat_hbm.at[s, :, lanes], mat_ref.at[s, q], sems.at[s, q])
        copy.start()
        copies.append(copy)
    return copies


def precond_kernel(sign_ref, msg_ref, mat_hbm, out_ref, x_ref, mat_ref, sems):
    copies = [load_columns(mat_hbm, s, mat_ref, sems) for s in range(2)]
    unpack_slots(msg_ref, x_ref)
    acc = jnp.zeros((CASES, 128), F32)
    for s in range(2):
        for q in range(3):
            copies[s][q].wait()
            y = jnp.dot(x_ref[s], mat_ref[s, q], preferred_element_type=F32)
            acc += lane_tiles(x_ref[s, :, pl.ds(512 * q, 512)].astype(F32) * y)
            send_rows(y, s, q, sign_ref, out_ref)
    send_sums(acc, out_ref)


def precond(sign, msg, mats):
    return pl.pallas_call(
        precond_kernel,
        out_shape=shape_of((N_DOM, 112, 128), BF16),
        in_specs=[SMEM_SPEC, VMEM_SPEC, HBM_SPEC],
        out_specs=VMEM_SPEC,
        scratch_shapes=[
            pltpu.VMEM((2, CASES, LOCAL), BF16),
            pltpu.VMEM((2, 3, LOCAL, 512), BF16),
            pltpu.SemaphoreType.DMA((2, 3)),
        ],
        compiler_params=params(52),
        name="precond",
    )(sign, msg, mats)


def tile_sums(msg_ref):
    total = jnp.zeros((16, 128), F32)
    for j in range(N_DOM):
        total += msg_ref[j].astype(F32)
    return total[:8] + total[8:]


def rho_kernel(msg_ref, ids_ref, out_ref):
    tile = tile_sums(msg_ref)
    for b in range(N_BLK):
        out_ref[b, pl.ds(0, 8), :] = tile
        out_ref[b, pl.ds(8, 8), :] = ids_ref[b]


def rho_parts(msg, ids):
    return pl.pallas_call(
        rho_kernel,
        grid=(1,),
        out_shape=shape_of((N_BLK, 16, 128), F32),
        in_specs=[pl.BlockSpec((N_DOM, 16, 128), lambda i: (0, 6, 0)), whole((N_BLK, 8, 128))],
        out_specs=whole((N_BLK, 16, 128)),
        compiler_params=params(),
        name="rho_parts",
    )(msg, ids)


def faces_kernel(place_ref, msg_ref, out_ref, both_ref):
    scatter_slots(msg_ref, place_ref, both_ref)
    out_ref[...] = both_ref[:COL_FACES] + both_ref[COL_FACES:]


def face_sums(place, msg):
    return pl.pallas_call(
        faces_kernel,
        out_shape=shape_of((COL_FACES, 8, 128), F32),
        in_specs=[SMEM_SPEC, VMEM_SPEC],
        out_specs=VMEM_SPEC,
        scratch_shapes=[pltpu.VMEM((COL_SLOTS, 8, 128), F32)],
        compiler_params=params(),
        name="face_sums",
    )(place, msg)


def all_of(parts_ref):
    return sum(parts_ref[b, pl.ds(0, 8), :] for b in range(N_BLK))


def direction_kernel(ids_ref, sign_ref, parts_ref, prev_ref, p_ref, msg_ref, out_ref, rho_ref, wide_ref):
    rho = jnp.sum(all_of(parts_ref), axis=1, keepdims=True) * (1.0 / TOTAL)
    rho_ref[...] = jnp.broadcast_to(rho, (8, 128))
    beta = jnp.broadcast_to(rho / prev_ref[:, :1], (8, 128))
    faces_wide(msg_ref, 48, wide_ref)
    wide_ref[...] = p_ref[...] + beta[None] * wide_ref[...]
    emit_slots(wide_ref, ids_ref, sign_ref, out_ref)


def directions(ids, sign, parts, prev, p, msg):
    return pl.pallas_call(
        direction_kernel,
        out_shape=(shape_of((N_DOM, 96, 128), BF16), shape_of((8, 128), F32)),
        in_specs=[SMEM_SPEC, SMEM_SPEC] + [VMEM_SPEC] * 4,
        out_specs=(VMEM_SPEC, VMEM_SPEC),
        scratch_shapes=[pltpu.VMEM((COL_FACES, 8, 128), F32)],
        compiler_params=params(),
        name="directions",
    )(ids, sign, parts, prev, p, msg)


def corner_kernel(msg_ref, coupling_ref, x_ref, out_ref):
    unpack_slots(msg_ref, x_ref)
    for s in range(2):
        terms = lax.dot_general(
            coupling_ref[s], x_ref[s], (((1,), (1,)), ((), ())), preferred_element_type=F32
        )
        for b in range(N_BLK):
            out_ref[b, :, pl.ds(64 * s, 64)] = terms[32 * b : 32 * b + 32].astype(BF16)


def corners(msg, coupling):
    return pl.pallas_call(
        corner_kernel,
        out_shape=(shape_of((2, CASES, LOCAL), BF16), shape_of((N_BLK, 32, 128), BF16)),
        in_specs=[VMEM_SPEC, VMEM_SPEC],
        out_specs=(VMEM_SPEC, VMEM_SPEC),
        compiler_params=params(),
        name="corners",
    )(msg, coupling)


def dual_kernel(s, x_ref, after_ref, mat_hbm, out_ref, mat_ref, sems):
    copies = load_columns(mat_hbm, s, mat_ref, sems)
    for q in range(3):
        copies[q].wait()
        out_ref[:, pl.ds(512 * q, 512)] = jnp.dot(x_ref[s], mat_ref[s, q], preferred_element_type=F32)


def dual(s, x, after, mats):
    return pl.pallas_call(
        functools.partial(dual_kernel, s),
        out_shape=shape_of((CASES, LOCAL), F32),
        in_specs=[VMEM_SPEC, HBM_SPEC, HBM_SPEC],
        out_specs=VMEM_SPEC,
        scratch_shapes=[
            pltpu.VMEM((2, 3, LOCAL, 512), BF16),
            pltpu.SemaphoreType.DMA((2, 3)),
        ],
        compiler_params=params(52),
        cost_estimate=pl.CostEstimate(
            flops=2 * CASES * LOCAL * LOCAL, bytes_accessed=2 * LOCAL * LOCAL, transcendentals=0
        ),
        name="dual",
    )(x, after, mats)


def matrix_kernel(parts_ref, after_ref, inv_ref, out_ref, hot_ref):
    lane = lax.broadcasted_iota(jnp.int32, (1, 128), 1) // 32
    spot = lax.broadcasted_iota(jnp.int32, (CB, 128), 0)
    for group in range(4):
        s, half = divmod(group, 2)
        ids = parts_ref[4 * half, pl.ds(8 + s, 1), :]
        for i in range(1, 4):
            ids = jnp.where(lane == i, parts_ref[4 * half + i, pl.ds(8 + s, 1), :], ids)
        hot = spot == jnp.broadcast_to(ids.astype(jnp.int32), (CB, 128))
        hot_ref[:, pl.ds(128 * group, 128)] = hot.astype(F32).astype(BF16)
    hot = hot_ref[...]
    columns = jnp.dot(inv_ref[...], hot, preferred_element_type=F32).astype(BF16)
    picked = lax.dot_general(hot, columns, (((0,), (0,)), ((), ())), preferred_element_type=F32)
    out_ref[...] = picked.astype(BF16)


def corner_matrix(parts, after, inv):
    return pl.pallas_call(
        matrix_kernel,
        out_shape=shape_of((512, 512), BF16),
        in_specs=[VMEM_SPEC, HBM_SPEC, VMEM_SPEC],
        out_specs=VMEM_SPEC,
        scratch_shapes=[pltpu.VMEM((CB, 512), BF16)],
        compiler_params=params(),
        cost_estimate=pl.CostEstimate(
            flops=2 * CB * 512 * (CB + 512), bytes_accessed=4 * CB * CB, transcendentals=0
        ),
        name="corner_matrix",
    )(parts, after, inv)


def solve_kernel(matrix_ref, terms_ref, out_ref, rhs_ref):
    terms = terms_ref[...].reshape(256, 128)
    rhs_ref[pl.ds(0, 256), :] = terms[:, :64]
    rhs_ref[pl.ds(256, 256), :] = terms[:, 64:]
    got = jnp.dot(matrix_ref[...], rhs_ref[...], preferred_element_type=F32).astype(BF16)
    for b in range(N_BLK):
        out_ref[b, :, pl.ds(0, 64)] = got[32 * b : 32 * b + 32]
        out_ref[b, :, pl.ds(64, 64)] = got[256 + 32 * b : 288 + 32 * b]


def solve(matrix, terms):
    return pl.pallas_call(
        solve_kernel,
        out_shape=shape_of((N_BLK, 32, 128), BF16),
        in_specs=[VMEM_SPEC, VMEM_SPEC],
        out_specs=VMEM_SPEC,
        scratch_shapes=[pltpu.VMEM((512, CASES), BF16)],
        compiler_params=params(),
        name="solve",
    )(matrix, terms)


def image_kernel(sign_ref, picks_ref, x_ref, first_ref, second_ref, coupling_ref, out_ref):
    picks = picks_ref[...].reshape(NCD, 128)
    acc = jnp.zeros((CASES, 128), F32)
    for s in range(2):
        coarse = lax.dot_general(
            picks[:, 64 * s : 64 * s + 64],
            coupling_ref[s],
            (((0,), (0,)), ((), ())),
            preferred_element_type=F32,
        )
        for q in range(3):
            lanes = slice(512 * q, 512 * q + 512)
            y = (first_ref, second_ref)[s][:, lanes] + coarse[:, lanes]
            acc += lane_tiles(x_ref[s, :, lanes].astype(F32) * y)
            send_rows(y, s, q, sign_ref, out_ref)
    send_sums(acc, out_ref)


def image_rows(sign, picks, x, first, second, coupling):
    return pl.pallas_call(
        image_kernel,
        out_shape=shape_of((N_DOM, 112, 128), BF16),
        in_specs=[SMEM_SPEC] + [VMEM_SPEC] * 5,
        out_specs=VMEM_SPEC,
        compiler_params=params(),
        name="image_rows",
    )(sign, picks, x, first, second, coupling)


def back_kernel(place_ref, at_ref, msg_ref, p_ref, first_ref, rho_ref, out_ref, both_ref):
    scatter_slots(msg_ref, place_ref, both_ref)
    total = jnp.zeros((16, 128), F32)
    for j in range(N_DOM):
        total += msg_ref[j, pl.ds(96, 16), :].astype(F32)
    s0 = jnp.zeros((8, 128), F32)
    s1 = jnp.zeros((8, 128), F32)
    s2 = jnp.zeros((8, 128), F32)
    for o in range(N_DOM):
        for q in range(FACES // 2):
            f = FACES * o + 2 * q
            one = both_ref[f] + both_ref[COL_FACES + f]
            two = both_ref[f + 1] + both_ref[COL_FACES + f + 1]
            res = first_ref[o, pl.ds(16 * q, 16), :].astype(F32)
            s0 += res[:8] * res[:8] + res[8:] * res[8:]
            s1 += res[:8] * one + res[8:] * two
            s2 += one * one + two * two
            out_ref[o, pl.ds(16 * q, 16), :] = pair(one, two).astype(BF16)
            out_ref[o, pl.ds(48 + 16 * q, 16), :] = pair(p_ref[f], p_ref[f + 1]).astype(BF16)
    base = at_ref[0]
    half = (1 - at_ref[1]).astype(F32)
    lane = lax.broadcasted_iota(jnp.int32, (8, 128), 1)
    stats = jnp.zeros((8, 128), F32)
    sums = (
        rho_ref[:, :1] * (half * (1.0 / N_BLK)),
        jnp.sum(total[:8] + total[8:], axis=1, keepdims=True) * half,
        jnp.sum(s0, axis=1, keepdims=True),
        jnp.sum(s1, axis=1, keepdims=True),
        jnp.sum(s2, axis=1, keepdims=True),
    )
    for k, value in enumerate(sums):
        value = jnp.broadcast_to(value, (8, 128))
        high, rest = split_two(value)
        stats = jnp.where(lane == base + k, high, stats)
        stats = jnp.where(lane == base + 64 + k, rest, stats)
    high, rest = split_two(stats)
    tile = pair(high, rest).astype(BF16)
    for o in range(N_DOM):
        out_ref[o, pl.ds(96, 16), :] = tile


def back(place, at, msg, p, first, rho):
    return pl.pallas_call(
        back_kernel,
        out_shape=shape_of((N_DOM, 112, 128), BF16),
        in_specs=[SMEM_SPEC, SMEM_SPEC] + [VMEM_SPEC] * 4,
        out_specs=VMEM_SPEC,
        scratch_shapes=[pltpu.VMEM((COL_SLOTS, 8, 128), F32)],
        compiler_params=params(),
        name="back",
    )(place, at, msg, p, first, rho)


def sums_kernel(msg_ref, out_ref):
    tile = tile_sums(msg_ref)
    for b in range(N_BLK):
        out_ref[b] = tile


def sums_parts(msg):
    return pl.pallas_call(
        sums_kernel,
        grid=(1,),
        out_shape=shape_of((N_BLK, 8, 128), F32),
        in_specs=[pl.BlockSpec((N_DOM, 16, 128), lambda i: (0, 6, 0))],
        out_specs=whole((N_BLK, 8, 128)),
        compiler_params=params(),
        name="sums_parts",
    )(msg)


def in_a_row(column):
    at_row = lax.broadcasted_iota(jnp.int32, (8, CASES), 0)
    at_lane = lax.broadcasted_iota(jnp.int32, (8, CASES), 1)
    row = jnp.zeros((1, CASES), F32)
    for g, value in enumerate(column):
        spread = jnp.where(at_lane == at_row + 8 * g, jnp.broadcast_to(value, (8, CASES)), 0.0)
        row += jnp.sum(spread, axis=0, keepdims=True)
    return row


def final_kernel(parts_ref, prev_ref, msg_ref, lam_ref, res_ref, dir_ref, lam_out, res_out, dir_out, rho_out, red_out):
    both = all_of(parts_ref)
    total = both[:, :64] + both[:, 64:]
    rho_now, reduction = [], []
    for g in range(8):
        rho = total[:, 8 * g : 8 * g + 1]
        curve = total[:, 8 * g + 1 : 8 * g + 2] * (1.0 / TOTAL)
        s0 = total[:, 8 * g + 2 : 8 * g + 3]
        s1 = total[:, 8 * g + 3 : 8 * g + 4]
        s2 = total[:, 8 * g + 4 : 8 * g + 5]
        alpha = rho / curve
        rows = pl.ds(8 * g, 8)
        beta = rho / prev_ref[rows, :]
        rho_now.append(rho)
        reduction.append((s0 - alpha * (2.0 * s1 - alpha * s2)) / s0)
        alpha = jnp.broadcast_to(alpha, (8, 128))
        beta = jnp.broadcast_to(beta, (8, 128))
        for h in range(2):
            lanes = pl.ds(128 * h, 128)
            for q in range(FACES // 2):
                image = msg_ref[2 * g + h, pl.ds(16 * q, 16), :].astype(F32)
                p = msg_ref[2 * g + h, pl.ds(48 + 16 * q, 16), :].astype(F32)
                for k in range(2):
                    f = 2 * q + k
                    half = slice(8 * k, 8 * k + 8)
                    direction = p[half] + beta * dir_ref[f, rows, lanes]
                    dir_out[f, rows, lanes] = direction
                    lam_out[f, rows, lanes] = lam_ref[f, rows, lanes] + alpha * direction
                    res_out[f, rows, lanes] = res_ref[f, rows, lanes] - alpha * image[half]
    rho_out[...] = in_a_row(rho_now)
    red_out[...] = in_a_row(reduction)


def final(parts, prev, msg, lam, res, dirp):
    field = shape_of((FACES, CASES, FDOF), F32)
    row = shape_of((1, CASES), F32)
    return pl.pallas_call(
        final_kernel,
        out_shape=(field, field, field, row, row),
        in_specs=[VMEM_SPEC] * 6,
        out_specs=(VMEM_SPEC,) * 5,
        compiler_params=params(),
        name="final",
    )(parts, prev, msg, lam, res, dirp)


def exchange(value, axis):
    return lax.all_to_all(value, axis, 0, 0, tiled=True)


def on_device(
    multipliers,
    residual,
    dir_prev,
    rho_prev,
    face_ids,
    face_sign,
    dual_blocks,
    dirichlet_blocks,
    coupling,
    corner_ids,
    coarse_inv,
):
    me = lax.axis_index(DOM)
    case_group = me // 2
    ids = face_ids[0].reshape(-1)
    sign_int = face_sign[0].reshape(-1)
    sign = sign_int.astype(F32)
    place = jnp.where(sign_int < 0, ids + COL_FACES, ids)
    my_sign = lax.dynamic_slice_in_dim(sign, me * SLOTS, SLOTS)
    at = jnp.stack([8 * case_group, me % 2]).astype(jnp.int32)
    block_ids = jnp.swapaxes(corner_ids[0].reshape(2, N_BLK, 32), 0, 1) - CB * jnp.arange(N_BLK)[:, None, None]
    block_ids = jnp.tile(block_ids.astype(F32), (1, 4, 4))
    prev = rho_prev[:, None]
    prev_mine = jnp.broadcast_to(lax.dynamic_slice_in_dim(prev, 8 * case_group, 8), (8, 128))

    first = exchange(pack(residual[0], dir_prev[0]), DOM)
    slots = exchange(pull(ids, sign, first), DOM)
    rows = exchange(precond(my_sign, slots, dirichlet_blocks[0]), DOM)
    parts = exchange(rho_parts(rows, block_ids), BLK)
    p = face_sums(place, rows)
    out_slots, rho = directions(ids, sign, parts, prev_mine, p, first)
    dir_slots = exchange(out_slots, DOM)
    matrix = corner_matrix(parts, rho, coarse_inv[0, 0])
    dir_slots, matrix = lax.optimization_barrier((dir_slots, matrix))
    x, terms = corners(dir_slots, coupling[0])
    dual_first = dual(0, x, rho, dual_blocks[0])
    terms = exchange(terms, BLK)
    terms, dual_first = lax.optimization_barrier((terms, dual_first))
    solved = solve(matrix, terms)
    dual_second = dual(1, x, solved, dual_blocks[0])
    picks = exchange(solved, BLK)
    image = exchange(
        image_rows(my_sign, picks, x, dual_first, dual_second, coupling[0]), DOM
    )
    msg = exchange(back(place, at, image, p, first, rho), DOM)
    sums = exchange(sums_parts(msg), BLK)
    lam, res, direction, rho_now, reduction = final(
        sums, prev, msg, multipliers[0], residual[0], dir_prev[0]
    )
    return (lam[None], res[None], direction[None], rho_now[0], reduction[0])


def solution(mesh):
    split = Mesh(mesh.devices.reshape(4, 4, 4, 2), ("dom_0", "dom_1", "blk_0", "blk_1"))
    in_specs = (
        P(BLK, DOM, None, None),
        P(BLK, DOM, None, None),
        P(BLK, DOM, None, None),
        P(),
        P(BLK, None, None),
        P(BLK, None, None),
        P(BLK, DOM, None, None),
        P(BLK, DOM, None, None),
        P(BLK, DOM, None, None),
        P(BLK, DOM, None),
        P(DOM, BLK, None, None),
    )
    out_specs = (
        P(BLK, DOM, None, None),
        P(BLK, DOM, None, None),
        P(BLK, DOM, None, None),
        P(),
        P(),
    )
    return jax.shard_map(
        on_device, mesh=split, in_specs=in_specs, out_specs=out_specs, check_vma=False
    )
```

```python
import functools

import jax
import jax.numpy as jnp
from jax import lax
from jax.experimental import pallas as pl
from jax.experimental.pallas import tpu as pltpu
from jax.sharding import Mesh
from jax.sharding import PartitionSpec as P

DOM = ("dom_0", "dom_1")
BLK = ("blk_0", "blk_1")

F32 = jnp.float32
BF16 = jnp.bfloat16

FACES = 6
SLOTS = 12
N_DOM = 16
N_BLK = 8
COL_FACES = FACES * N_DOM
COL_SLOTS = SLOTS * N_DOM
CASES = 64
FDOF = 256
LOCAL = 1536
NCD = 256
CB = 768
TOTAL = float(N_BLK * COL_FACES * FDOF)


VMEM_SPEC = pl.BlockSpec(memory_space=pltpu.VMEM)
SMEM_SPEC = pl.BlockSpec(memory_space=pltpu.SMEM)
HBM_SPEC = pl.BlockSpec(memory_space=pl.ANY)


def whole(shape):
    return pl.BlockSpec(shape, lambda *_: (0,) * len(shape))


def params(mib=16):
    return pltpu.CompilerParams(vmem_limit_bytes=mib * 1024 * 1024)


def shape_of(shape, dtype):
    return jax.ShapeDtypeStruct(shape, dtype)


def pair(a, b):
    return jnp.concatenate([a, b], axis=0)


def split_two(tile):
    high = tile.astype(BF16).astype(F32)
    return high, tile - high


def pack_kernel(res_hbm, dir_hbm, out_ref, field_ref, sems):
    copies = []
    for kind, hbm in enumerate((res_hbm, dir_hbm)):
        for q in range(FACES // 2):
            copy = pltpu.make_async_copy(
                hbm.at[pl.ds(2 * q, 2)], field_ref.at[kind, pl.ds(2 * q, 2)], sems.at[kind, q]
            )
            copy.start()
            copies.append((kind, q, copy))
    for kind, q, copy in copies:
        copy.wait()
        for g in range(8):
            for h in range(2):
                rows, lanes = pl.ds(8 * g, 8), pl.ds(128 * h, 128)
                tile = pair(field_ref[kind, 2 * q, rows, lanes], field_ref[kind, 2 * q + 1, rows, lanes])
                out_ref[2 * g + h, pl.ds(kind * 48 + 16 * q, 16), :] = tile.astype(BF16)


def pack(res, dirp):
    return pl.pallas_call(
        pack_kernel,
        out_shape=shape_of((N_DOM, 96, 128), BF16),
        in_specs=[HBM_SPEC, HBM_SPEC],
        out_specs=VMEM_SPEC,
        scratch_shapes=[
            pltpu.VMEM((2, FACES, CASES, FDOF), F32),
            pltpu.SemaphoreType.DMA((2, FACES // 2)),
        ],
        compiler_params=params(58),
        name="pack",
    )(res, dirp)


def faces_wide(msg_ref, first, wide_ref):
    for o in range(N_DOM):
        for q in range(FACES // 2):
            tile = msg_ref[o, pl.ds(first + 16 * q, 16), :].astype(F32)
            wide_ref[FACES * o + 2 * q] = tile[:8]
            wide_ref[FACES * o + 2 * q + 1] = tile[8:]


def emit_slots(wide_ref, ids_ref, sign_ref, out_ref):
    for j in range(N_DOM):
        for q in range(SLOTS // 2):
            e = SLOTS * j + 2 * q
            tile = pair(
                wide_ref[ids_ref[e]] * sign_ref[e],
                wide_ref[ids_ref[e + 1]] * sign_ref[e + 1],
            )
            out_ref[j, pl.ds(16 * q, 16), :] = tile.astype(BF16)


def scatter_slots(msg_ref, place_ref, both_ref):
    for j in range(N_DOM):
        for q in range(SLOTS // 2):
            e = SLOTS * j + 2 * q
            tile = msg_ref[j, pl.ds(16 * q, 16), :].astype(F32)
            both_ref[place_ref[e]] = tile[:8]
            both_ref[place_ref[e + 1]] = tile[8:]


def pull_kernel(ids_ref, sign_ref, msg_ref, out_ref, wide_ref):
    faces_wide(msg_ref, 0, wide_ref)
    emit_slots(wide_ref, ids_ref, sign_ref, out_ref)


def pull(ids, sign, msg):
    return pl.pallas_call(
        pull_kernel,
        out_shape=shape_of((N_DOM, 96, 128), BF16),
        in_specs=[SMEM_SPEC, SMEM_SPEC, VMEM_SPEC],
        out_specs=VMEM_SPEC,
        scratch_shapes=[pltpu.VMEM((COL_FACES, 8, 128), F32)],
        compiler_params=params(),
        name="pull",
    )(ids, sign, msg)


def unpack_slots(msg_ref, x_ref):
    for m in range(4):
        for h in range(2):
            for q6 in range(6):
                s, q = divmod(q6, 3)
                upper = msg_ref[4 * m + h, pl.ds(16 * q6, 16), :].astype(F32)
                lower = msg_ref[4 * m + 2 + h, pl.ds(16 * q6, 16), :].astype(F32)
                rows = pl.ds(16 * m, 16)
                x_ref[s, rows, pl.ds(512 * q + 128 * h, 128)] = pair(upper[:8], lower[:8]).astype(BF16)
                x_ref[s, rows, pl.ds(512 * q + 256 + 128 * h, 128)] = pair(upper[8:], lower[8:]).astype(BF16)


def send_rows(y, s, q, sign_ref, out_ref):
    first = sign_ref[6 * s + 2 * q]
    second = sign_ref[6 * s + 2 * q + 1]
    start = (3 * s + q) * 16
    for g in range(8):
        for h in range(2):
            tile = pair(
                y[8 * g : 8 * g + 8, 128 * h : 128 * h + 128] * first,
                y[8 * g : 8 * g + 8, 256 + 128 * h : 384 + 128 * h] * second,
            )
            out_ref[2 * g + h, pl.ds(start, 16), :] = tile.astype(BF16)


def lane_tiles(v):
    return sum(v[:, 128 * k : 128 * k + 128] for k in range(4))


def send_sums(acc, out_ref):
    high, low = split_two(acc)
    for g in range(8):
        tile = pair(high[8 * g : 8 * g + 8], low[8 * g : 8 * g + 8]).astype(BF16)
        for h in range(2):
            out_ref[2 * g + h, pl.ds(96, 16), :] = tile


def load_columns(mat_hbm, mat_ref, sems):
    copies = []
    for q in range(3):
        copy = pltpu.make_async_copy(mat_hbm.at[:, pl.ds(512 * q, 512)], mat_ref.at[q], sems.at[q])
        copy.start()
        copies.append(copy)
    return copies


def precond_kernel(sign_ref, msg_ref, mat_hbm, out_ref, x_ref, mat_ref, sems):
    copies = [load_columns(mat_hbm.at[s], mat_ref.at[s], sems.at[s]) for s in range(2)]
    unpack_slots(msg_ref, x_ref)
    acc = jnp.zeros((CASES, 128), F32)
    for s in range(2):
        for q in range(3):
            copies[s][q].wait()
            y = jnp.dot(x_ref[s], mat_ref[s, q], preferred_element_type=F32)
            acc += lane_tiles(x_ref[s, :, pl.ds(512 * q, 512)].astype(F32) * y)
            send_rows(y, s, q, sign_ref, out_ref)
    send_sums(acc, out_ref)


def precond(sign, msg, mats):
    return pl.pallas_call(
        precond_kernel,
        out_shape=shape_of((N_DOM, 112, 128), BF16),
        in_specs=[SMEM_SPEC, VMEM_SPEC, HBM_SPEC],
        out_specs=VMEM_SPEC,
        scratch_shapes=[
            pltpu.VMEM((2, CASES, LOCAL), BF16),
            pltpu.VMEM((2, 3, LOCAL, 512), BF16),
            pltpu.SemaphoreType.DMA((2, 3)),
        ],
        compiler_params=params(52),
        name="precond",
    )(sign, msg, mats)


def tile_sums(msg_ref):
    total = jnp.zeros((16, 128), F32)
    for j in range(N_DOM):
        total += msg_ref[j].astype(F32)
    return total[:8] + total[8:]


def rho_kernel(msg_ref, ids_ref, out_ref):
    tile = tile_sums(msg_ref)
    for b in range(N_BLK):
        out_ref[b, pl.ds(0, 8), :] = tile
        out_ref[b, pl.ds(8, 8), :] = ids_ref[b]


def rho_parts(msg, ids):
    return pl.pallas_call(
        rho_kernel,
        grid=(1,),
        out_shape=shape_of((N_BLK, 16, 128), F32),
        in_specs=[pl.BlockSpec((N_DOM, 16, 128), lambda i: (0, 6, 0)), whole((N_BLK, 8, 128))],
        out_specs=whole((N_BLK, 16, 128)),
        compiler_params=params(),
        name="rho_parts",
    )(msg, ids)


def faces_kernel(place_ref, msg_ref, out_ref, both_ref):
    scatter_slots(msg_ref, place_ref, both_ref)
    out_ref[...] = both_ref[:COL_FACES] + both_ref[COL_FACES:]


def face_sums(place, msg):
    return pl.pallas_call(
        faces_kernel,
        out_shape=shape_of((COL_FACES, 8, 128), F32),
        in_specs=[SMEM_SPEC, VMEM_SPEC],
        out_specs=VMEM_SPEC,
        scratch_shapes=[pltpu.VMEM((COL_SLOTS, 8, 128), F32)],
        compiler_params=params(),
        name="face_sums",
    )(place, msg)


def all_of(parts_ref):
    return sum(parts_ref[b, pl.ds(0, 8), :] for b in range(N_BLK))


def direction_kernel(ids_ref, sign_ref, parts_ref, prev_ref, p_ref, msg_ref, out_ref, rho_ref, wide_ref):
    rho = jnp.sum(all_of(parts_ref), axis=1, keepdims=True) * (1.0 / TOTAL)
    rho_ref[...] = jnp.broadcast_to(rho, (8, 128))
    beta = jnp.broadcast_to(rho / prev_ref[:, :1], (8, 128))
    faces_wide(msg_ref, 48, wide_ref)
    wide_ref[...] = p_ref[...] + beta[None] * wide_ref[...]
    emit_slots(wide_ref, ids_ref, sign_ref, out_ref)


def directions(ids, sign, parts, prev, p, msg):
    return pl.pallas_call(
        direction_kernel,
        out_shape=(shape_of((N_DOM, 96, 128), BF16), shape_of((8, 128), F32)),
        in_specs=[SMEM_SPEC, SMEM_SPEC] + [VMEM_SPEC] * 4,
        out_specs=(VMEM_SPEC, VMEM_SPEC),
        scratch_shapes=[pltpu.VMEM((COL_FACES, 8, 128), F32)],
        compiler_params=params(),
        name="directions",
    )(ids, sign, parts, prev, p, msg)


def corner_kernel(msg_ref, coupling_ref, x_ref, out_ref):
    unpack_slots(msg_ref, x_ref)
    for s in range(2):
        terms = lax.dot_general(
            coupling_ref[s], x_ref[s], (((1,), (1,)), ((), ())), preferred_element_type=F32
        )
        for b in range(N_BLK):
            out_ref[b, :, pl.ds(64 * s, 64)] = terms[32 * b : 32 * b + 32].astype(BF16)


def corners(msg, coupling):
    return pl.pallas_call(
        corner_kernel,
        out_shape=(shape_of((2, CASES, LOCAL), BF16), shape_of((N_BLK, 32, 128), BF16)),
        in_specs=[VMEM_SPEC, VMEM_SPEC],
        out_specs=(VMEM_SPEC, VMEM_SPEC),
        compiler_params=params(),
        name="corners",
    )(msg, coupling)


def dual_kernel(x_ref, mat_hbm, out_ref, sum_ref, mat_ref, sems):
    copies = [load_columns(mat_hbm.at[s], mat_ref.at[s], sems.at[s]) for s in range(2)]
    acc = jnp.zeros((CASES, 128), F32)
    for s in range(2):
        for q in range(3):
            copies[s][q].wait()
            lanes = pl.ds(512 * q, 512)
            y = jnp.dot(x_ref[s], mat_ref[s, q], preferred_element_type=F32)
            out_ref[s, :, lanes] = y
            acc += lane_tiles(x_ref[s, :, lanes].astype(F32) * y)
    sum_ref[...] = acc


def dual(x, mats):
    return pl.pallas_call(
        dual_kernel,
        out_shape=(shape_of((2, CASES, LOCAL), F32), shape_of((CASES, 128), F32)),
        in_specs=[VMEM_SPEC, HBM_SPEC],
        out_specs=(VMEM_SPEC, VMEM_SPEC),
        scratch_shapes=[
            pltpu.VMEM((2, 3, LOCAL, 512), BF16),
            pltpu.SemaphoreType.DMA((2, 3)),
        ],
        compiler_params=params(52),
        cost_estimate=pl.CostEstimate(
            flops=4 * CASES * LOCAL * LOCAL, bytes_accessed=4 * LOCAL * LOCAL, transcendentals=0
        ),
        name="dual",
    )(x, mats)


def matrix_kernel(parts_ref, after_ref, inv_ref, out_ref, hot_ref):
    lane = lax.broadcasted_iota(jnp.int32, (1, 128), 1) // 32
    spot = lax.broadcasted_iota(jnp.int32, (CB, 128), 0)
    for group in range(4):
        s, half = divmod(group, 2)
        ids = parts_ref[4 * half, pl.ds(8 + s, 1), :]
        for i in range(1, 4):
            ids = jnp.where(lane == i, parts_ref[4 * half + i, pl.ds(8 + s, 1), :], ids)
        hot = spot == jnp.broadcast_to(ids.astype(jnp.int32), (CB, 128))
        hot_ref[:, pl.ds(128 * group, 128)] = hot.astype(F32).astype(BF16)
    hot = hot_ref[...]
    columns = jnp.dot(inv_ref[...], hot, preferred_element_type=F32).astype(BF16)
    picked = lax.dot_general(hot, columns, (((0,), (0,)), ((), ())), preferred_element_type=F32)
    out_ref[...] = picked.astype(BF16)


def corner_matrix(parts, after, inv):
    return pl.pallas_call(
        matrix_kernel,
        out_shape=shape_of((512, 512), BF16),
        in_specs=[VMEM_SPEC, HBM_SPEC, VMEM_SPEC],
        out_specs=VMEM_SPEC,
        scratch_shapes=[pltpu.VMEM((CB, 512), BF16)],
        compiler_params=params(),
        cost_estimate=pl.CostEstimate(
            flops=2 * CB * 512 * (CB + 512), bytes_accessed=4 * CB * CB, transcendentals=0
        ),
        name="corner_matrix",
    )(parts, after, inv)


def lane_of(index):
    return lax.broadcasted_iota(jnp.int32, (8, 128), 1) == index


def packed(columns, base):
    stats = jnp.zeros((8, 128), F32)
    for k, value in enumerate(columns):
        high, rest = split_two(jnp.broadcast_to(value, (8, 128)))
        stats = jnp.where(lane_of(base + k), high, stats)
        stats = jnp.where(lane_of(base + 64 + k), rest, stats)
    high, rest = split_two(stats)
    return pair(high, rest).astype(BF16)


def solve_kernel(matrix_ref, terms_ref, sum_ref, out_ref, rhs_ref):
    terms = terms_ref[...].reshape(256, 128)
    rhs_ref[pl.ds(0, 256), :] = terms[:, :64]
    rhs_ref[pl.ds(256, 256), :] = terms[:, 64:]
    got = jnp.dot(matrix_ref[...], rhs_ref[...], preferred_element_type=F32).astype(BF16)
    for b in range(N_BLK):
        out_ref[b, pl.ds(0, 32), pl.ds(0, 64)] = got[32 * b : 32 * b + 32]
        out_ref[b, pl.ds(0, 32), pl.ds(64, 64)] = got[256 + 32 * b : 288 + 32 * b]
    coarse = jnp.sum(rhs_ref[...].astype(F32) * got.astype(F32), axis=0, keepdims=True)
    coarse = jnp.broadcast_to(coarse, (8, CASES))
    at_row = lax.broadcasted_iota(jnp.int32, (8, CASES), 0)
    at_lane = lax.broadcasted_iota(jnp.int32, (8, CASES), 1)
    columns = []
    for g in range(8):
        rows = pl.ds(8 * g, 8)
        value = jnp.sum(sum_ref[rows, :], axis=1, keepdims=True)
        spread = jnp.where(at_lane == at_row + 8 * g, coarse, 0.0)
        columns.append(value + jnp.sum(spread, axis=1, keepdims=True))
    tile = packed(columns, 0)
    for b in range(N_BLK):
        out_ref[b, pl.ds(32, 16), :] = tile


def solve(matrix, terms, sums):
    return pl.pallas_call(
        solve_kernel,
        out_shape=shape_of((N_BLK, 48, 128), BF16),
        in_specs=[VMEM_SPEC] * 3,
        out_specs=VMEM_SPEC,
        scratch_shapes=[pltpu.VMEM((512, CASES), BF16)],
        compiler_params=params(),
        name="solve",
    )(matrix, terms, sums)


def image_kernel(sign_ref, picks_ref, dual_ref, coupling_ref, out_ref):
    picks = picks_ref[:, pl.ds(0, 32), :].reshape(NCD, 128)
    for s in range(2):
        coarse = lax.dot_general(
            picks[:, 64 * s : 64 * s + 64],
            coupling_ref[s],
            (((0,), (0,)), ((), ())),
            preferred_element_type=F32,
        )
        for q in range(3):
            lanes = slice(512 * q, 512 * q + 512)
            y = dual_ref[s, :, lanes] + coarse[:, lanes]
            send_rows(y, s, q, sign_ref, out_ref)
    total = jnp.zeros((16, 128), F32)
    for b in range(N_BLK):
        total += picks_ref[b, pl.ds(32, 16), :].astype(F32)
    high, low = split_two(total[:8] + total[8:])
    tile = pair(high, low).astype(BF16)
    for i in range(N_DOM):
        out_ref[i, pl.ds(96, 16), :] = tile


def image_rows(sign, picks, dual_y, coupling):
    return pl.pallas_call(
        image_kernel,
        out_shape=shape_of((N_DOM, 112, 128), BF16),
        in_specs=[SMEM_SPEC] + [VMEM_SPEC] * 3,
        out_specs=VMEM_SPEC,
        compiler_params=params(),
        name="image_rows",
    )(sign, picks, dual_y, coupling)


def back_kernel(place_ref, at_ref, msg_ref, p_ref, first_ref, rho_ref, out_ref, both_ref):
    scatter_slots(msg_ref, place_ref, both_ref)
    total = jnp.zeros((16, 128), F32)
    for j in range(N_DOM):
        total += msg_ref[j, pl.ds(96, 16), :].astype(F32)
    base = at_ref[0]
    half = (1 - at_ref[1]).astype(F32)
    both = total[:8] + total[8:]
    lane8 = lax.broadcasted_iota(jnp.int32, (8, CASES), 1) * 8
    mine = jnp.where(lane8 == base, both[:, :64] + both[:, 64:], 0.0)
    curve = jnp.sum(mine, axis=1, keepdims=True) * (1.0 / TOTAL)
    rho = rho_ref[:, :1]
    alpha = rho / curve
    wide = jnp.broadcast_to(alpha, (8, 128))
    s0 = jnp.zeros((8, 128), F32)
    s2 = jnp.zeros((8, 128), F32)
    for o in range(N_DOM):
        for q in range(FACES // 2):
            f = FACES * o + 2 * q
            one = both_ref[f] + both_ref[COL_FACES + f]
            two = both_ref[f + 1] + both_ref[COL_FACES + f + 1]
            res = first_ref[o, pl.ds(16 * q, 16), :].astype(F32)
            new_one = res[:8] - wide * one
            new_two = res[8:] - wide * two
            s0 += res[:8] * res[:8] + res[8:] * res[8:]
            s2 += new_one * new_one + new_two * new_two
            out_ref[o, pl.ds(16 * q, 16), :] = pair(one, two).astype(BF16)
            out_ref[o, pl.ds(48 + 16 * q, 16), :] = pair(p_ref[f], p_ref[f + 1]).astype(BF16)
    sums = (
        rho * half,
        alpha * half,
        jnp.sum(s0, axis=1, keepdims=True),
        jnp.sum(s2, axis=1, keepdims=True),
    )
    tile = packed(sums, base)
    for o in range(N_DOM):
        out_ref[o, pl.ds(96, 16), :] = tile


def back(place, at, msg, p, first, rho):
    return pl.pallas_call(
        back_kernel,
        out_shape=shape_of((N_DOM, 112, 128), BF16),
        in_specs=[SMEM_SPEC, SMEM_SPEC] + [VMEM_SPEC] * 4,
        out_specs=VMEM_SPEC,
        scratch_shapes=[pltpu.VMEM((COL_SLOTS, 8, 128), F32)],
        compiler_params=params(),
        name="back",
    )(place, at, msg, p, first, rho)


def sums_kernel(msg_ref, out_ref):
    tile = tile_sums(msg_ref)
    for b in range(N_BLK):
        out_ref[b] = tile


def sums_parts(msg):
    return pl.pallas_call(
        sums_kernel,
        grid=(1,),
        out_shape=shape_of((N_BLK, 8, 128), F32),
        in_specs=[pl.BlockSpec((N_DOM, 16, 128), lambda i: (0, 6, 0))],
        out_specs=whole((N_BLK, 8, 128)),
        compiler_params=params(),
        name="sums_parts",
    )(msg)


def in_a_row(column):
    at_row = lax.broadcasted_iota(jnp.int32, (8, CASES), 0)
    at_lane = lax.broadcasted_iota(jnp.int32, (8, CASES), 1)
    row = jnp.zeros((1, CASES), F32)
    for g, value in enumerate(column):
        spread = jnp.where(at_lane == at_row + 8 * g, jnp.broadcast_to(value, (8, CASES)), 0.0)
        row += jnp.sum(spread, axis=0, keepdims=True)
    return row


def final_kernel(stats_ref, prev_ref, msg_ref, lam_ref, res_ref, dir_ref, lam_out, res_out, dir_out, rho_out):
    total = stats_ref[0, :, :64] + stats_ref[0, :, 64:]
    rho_now = []
    for g in range(8):
        rho = total[:, 8 * g : 8 * g + 1]
        rho_now.append(rho)
        rows = pl.ds(8 * g, 8)
        alpha = jnp.broadcast_to(total[:, 8 * g + 1 : 8 * g + 2], (8, 128))
        beta = jnp.broadcast_to(rho / prev_ref[rows, :], (8, 128))
        for h in range(2):
            lanes = pl.ds(128 * h, 128)
            for q in range(FACES // 2):
                image = msg_ref[2 * g + h, pl.ds(16 * q, 16), :].astype(F32)
                p = msg_ref[2 * g + h, pl.ds(48 + 16 * q, 16), :].astype(F32)
                for k in range(2):
                    f = 2 * q + k
                    half = slice(8 * k, 8 * k + 8)
                    direction = p[half] + beta * dir_ref[f, rows, lanes]
                    dir_out[f, rows, lanes] = direction
                    lam_out[f, rows, lanes] = lam_ref[f, rows, lanes] + alpha * direction
                    res_out[f, rows, lanes] = res_ref[f, rows, lanes] - alpha * image[half]
    rho_out[...] = in_a_row(rho_now)


def final(stats, prev, msg, lam, res, dirp):
    field = shape_of((FACES, CASES, FDOF), F32)
    return pl.pallas_call(
        final_kernel,
        out_shape=(field, field, field, shape_of((1, CASES), F32)),
        in_specs=[VMEM_SPEC] * 6,
        out_specs=(VMEM_SPEC,) * 4,
        compiler_params=params(),
        cost_estimate=pl.CostEstimate(
            flops=8 * FACES * CASES * FDOF, bytes_accessed=28 * FACES * CASES * FDOF, transcendentals=0
        ),
        name="final",
    )(stats, prev, msg, lam, res, dirp)


def reduction_kernel(parts_ref, out_ref):
    both = all_of(parts_ref)
    total = both[:, :64] + both[:, 64:]
    columns = [
        total[:, 8 * g + 3 : 8 * g + 4] / total[:, 8 * g + 2 : 8 * g + 3] for g in range(8)
    ]
    out_ref[...] = in_a_row(columns)


def reductions(parts):
    return pl.pallas_call(
        reduction_kernel,
        out_shape=shape_of((1, CASES), F32),
        in_specs=[VMEM_SPEC],
        out_specs=VMEM_SPEC,
        compiler_params=params(),
        name="reductions",
    )(parts)


def exchange(value, axis):
    return lax.all_to_all(value, axis, 0, 0, tiled=True)


def on_device(
    multipliers,
    residual,
    dir_prev,
    rho_prev,
    face_ids,
    face_sign,
    dual_blocks,
    dirichlet_blocks,
    coupling,
    corner_ids,
    coarse_inv,
):
    me = lax.axis_index(DOM)
    case_group = me // 2
    ids = face_ids[0].reshape(-1)
    sign_int = face_sign[0].reshape(-1)
    sign = sign_int.astype(F32)
    place = jnp.where(sign_int < 0, ids + COL_FACES, ids)
    my_sign = lax.dynamic_slice_in_dim(sign, me * SLOTS, SLOTS)
    at = jnp.stack([8 * case_group, me % 2]).astype(jnp.int32)
    block_ids = jnp.swapaxes(corner_ids[0].reshape(2, N_BLK, 32), 0, 1) - CB * jnp.arange(N_BLK)[:, None, None]
    block_ids = jnp.tile(block_ids.astype(F32), (1, 4, 4))
    prev = rho_prev[:, None]
    prev_mine = jnp.broadcast_to(lax.dynamic_slice_in_dim(prev, 8 * case_group, 8), (8, 128))

    first = exchange(pack(residual[0], dir_prev[0]), DOM)
    slots = exchange(pull(ids, sign, first), DOM)
    rows = exchange(precond(my_sign, slots, dirichlet_blocks[0]), DOM)
    parts = exchange(rho_parts(rows, block_ids), BLK)
    p = face_sums(place, rows)
    out_slots, rho = directions(ids, sign, parts, prev_mine, p, first)
    dir_slots = exchange(out_slots, DOM)
    matrix = corner_matrix(parts, rho, coarse_inv[0, 0])
    dir_slots, matrix = lax.optimization_barrier((dir_slots, matrix))
    x, terms = corners(dir_slots, coupling[0])
    dual_y, dual_sums = dual(x, dual_blocks[0])
    terms = exchange(terms, BLK)
    picks = exchange(solve(matrix, terms, dual_sums), BLK)
    image = exchange(image_rows(my_sign, picks, dual_y, coupling[0]), DOM)
    msg = exchange(back(place, at, image, p, first, rho), DOM)
    stats = sums_parts(msg)
    lam, res, direction, rho_now = final(stats, prev, msg, multipliers[0], residual[0], dir_prev[0])
    reduction = reductions(exchange(stats, BLK))
    return (lam[None], res[None], direction[None], rho_now[0], reduction[0])


def solution(mesh):
    split = Mesh(mesh.devices.reshape(4, 4, 4, 2), ("dom_0", "dom_1", "blk_0", "blk_1"))
    in_specs = (
        P(BLK, DOM, None, None),
        P(BLK, DOM, None, None),
        P(BLK, DOM, None, None),
        P(),
        P(BLK, None, None),
        P(BLK, None, None),
        P(BLK, DOM, None, None),
        P(BLK, DOM, None, None),
        P(BLK, DOM, None, None),
        P(BLK, DOM, None),
        P(DOM, BLK, None, None),
    )
    out_specs = (
        P(BLK, DOM, None, None),
        P(BLK, DOM, None, None),
        P(BLK, DOM, None, None),
        P(),
        P(),
    )
    return jax.shard_map(
        on_device, mesh=split, in_specs=in_specs, out_specs=out_specs, check_vma=False
    )
```

```python
import functools

import jax
import jax.numpy as jnp
from jax import lax
from jax.experimental import pallas as pl
from jax.experimental.pallas import tpu as pltpu
from jax.sharding import Mesh
from jax.sharding import PartitionSpec as P

DOM = ("dom_0", "dom_1")
BLK = ("blk_0", "blk_1")

F32 = jnp.float32
BF16 = jnp.bfloat16

FACES = 6
SLOTS = 12
N_DOM = 16
N_BLK = 8
COL_FACES = FACES * N_DOM
COL_SLOTS = SLOTS * N_DOM
CASES = 64
FDOF = 256
LOCAL = 1536
NCD = 256
CB = 768
TOTAL = float(N_BLK * COL_FACES * FDOF)


VMEM_SPEC = pl.BlockSpec(memory_space=pltpu.VMEM)
SMEM_SPEC = pl.BlockSpec(memory_space=pltpu.SMEM)
HBM_SPEC = pl.BlockSpec(memory_space=pl.ANY)


def whole(shape):
    return pl.BlockSpec(shape, lambda *_: (0,) * len(shape))


def params(mib=16):
    return pltpu.CompilerParams(vmem_limit_bytes=mib * 1024 * 1024)


def shape_of(shape, dtype):
    return jax.ShapeDtypeStruct(shape, dtype)


def pair(a, b):
    return jnp.concatenate([a, b], axis=0)


def split_two(tile):
    high = tile.astype(BF16).astype(F32)
    return high, tile - high


def pack_kernel(res_hbm, dir_hbm, out_ref, field_ref, sems):
    copies = []
    for kind, hbm in enumerate((res_hbm, dir_hbm)):
        for q in range(FACES // 2):
            copy = pltpu.make_async_copy(
                hbm.at[pl.ds(2 * q, 2)], field_ref.at[kind, pl.ds(2 * q, 2)], sems.at[kind, q]
            )
            copy.start()
            copies.append((kind, q, copy))
    for kind, q, copy in copies:
        copy.wait()
        for g in range(8):
            for h in range(2):
                rows, lanes = pl.ds(8 * g, 8), pl.ds(128 * h, 128)
                tile = pair(field_ref[kind, 2 * q, rows, lanes], field_ref[kind, 2 * q + 1, rows, lanes])
                out_ref[2 * g + h, pl.ds(kind * 48 + 16 * q, 16), :] = tile.astype(BF16)


def pack(res, dirp):
    return pl.pallas_call(
        pack_kernel,
        out_shape=shape_of((N_DOM, 96, 128), BF16),
        in_specs=[HBM_SPEC, HBM_SPEC],
        out_specs=VMEM_SPEC,
        scratch_shapes=[
            pltpu.VMEM((2, FACES, CASES, FDOF), F32),
            pltpu.SemaphoreType.DMA((2, FACES // 2)),
        ],
        compiler_params=params(58),
        name="pack",
    )(res, dirp)


def faces_wide(msg_ref, first, wide_ref):
    for o in range(N_DOM):
        for q in range(FACES // 2):
            tile = msg_ref[o, pl.ds(first + 16 * q, 16), :].astype(F32)
            wide_ref[FACES * o + 2 * q] = tile[:8]
            wide_ref[FACES * o + 2 * q + 1] = tile[8:]


def emit_slots(wide_ref, ids_ref, sign_ref, out_ref):
    for j in range(N_DOM):
        for q in range(SLOTS // 2):
            e = SLOTS * j + 2 * q
            tile = pair(
                wide_ref[ids_ref[e]] * sign_ref[e],
                wide_ref[ids_ref[e + 1]] * sign_ref[e + 1],
            )
            out_ref[j, pl.ds(16 * q, 16), :] = tile.astype(BF16)


def scatter_slots(msg_ref, place_ref, both_ref):
    for j in range(N_DOM):
        for q in range(SLOTS // 2):
            e = SLOTS * j + 2 * q
            tile = msg_ref[j, pl.ds(16 * q, 16), :].astype(F32)
            both_ref[place_ref[e]] = tile[:8]
            both_ref[place_ref[e + 1]] = tile[8:]


def pull_kernel(ids_ref, sign_ref, msg_ref, out_ref, wide_ref):
    faces_wide(msg_ref, 0, wide_ref)
    emit_slots(wide_ref, ids_ref, sign_ref, out_ref)


def pull(ids, sign, msg):
    return pl.pallas_call(
        pull_kernel,
        out_shape=shape_of((N_DOM, 96, 128), BF16),
        in_specs=[SMEM_SPEC, SMEM_SPEC, VMEM_SPEC],
        out_specs=VMEM_SPEC,
        scratch_shapes=[pltpu.VMEM((COL_FACES, 8, 128), F32)],
        compiler_params=params(),
        name="pull",
    )(ids, sign, msg)


def unpack_slots(msg_ref, x_ref):
    for m in range(4):
        for h in range(2):
            for q6 in range(6):
                s, q = divmod(q6, 3)
                upper = msg_ref[4 * m + h, pl.ds(16 * q6, 16), :].astype(F32)
                lower = msg_ref[4 * m + 2 + h, pl.ds(16 * q6, 16), :].astype(F32)
                rows = pl.ds(16 * m, 16)
                x_ref[s, rows, pl.ds(512 * q + 128 * h, 128)] = pair(upper[:8], lower[:8]).astype(BF16)
                x_ref[s, rows, pl.ds(512 * q + 256 + 128 * h, 128)] = pair(upper[8:], lower[8:]).astype(BF16)


def send_rows(y, s, q, sign_ref, out_ref):
    first = sign_ref[6 * s + 2 * q]
    second = sign_ref[6 * s + 2 * q + 1]
    start = (3 * s + q) * 16
    for g in range(8):
        for h in range(2):
            tile = pair(
                y[8 * g : 8 * g + 8, 128 * h : 128 * h + 128] * first,
                y[8 * g : 8 * g + 8, 256 + 128 * h : 384 + 128 * h] * second,
            )
            out_ref[2 * g + h, pl.ds(start, 16), :] = tile.astype(BF16)


def lane_tiles(v):
    return sum(v[:, 128 * k : 128 * k + 128] for k in range(4))


def send_sums(acc, out_ref):
    high, low = split_two(acc)
    for g in range(8):
        tile = pair(high[8 * g : 8 * g + 8], low[8 * g : 8 * g + 8]).astype(BF16)
        for h in range(2):
            out_ref[2 * g + h, pl.ds(96, 16), :] = tile


def load_columns(mat_hbm, mat_ref, sems):
    copies = []
    for q in range(3):
        copy = pltpu.make_async_copy(mat_hbm.at[:, pl.ds(512 * q, 512)], mat_ref.at[q], sems.at[q])
        copy.start()
        copies.append(copy)
    return copies


def precond_kernel(sign_ref, msg_ref, mat_hbm, out_ref, x_ref, mat_ref, sems):
    copies = [load_columns(mat_hbm.at[s], mat_ref.at[s], sems.at[s]) for s in range(2)]
    unpack_slots(msg_ref, x_ref)
    acc = jnp.zeros((CASES, 128), F32)
    for s in range(2):
        for q in range(3):
            copies[s][q].wait()
            y = jnp.dot(x_ref[s], mat_ref[s, q], preferred_element_type=F32)
            acc += lane_tiles(x_ref[s, :, pl.ds(512 * q, 512)].astype(F32) * y)
            send_rows(y, s, q, sign_ref, out_ref)
    send_sums(acc, out_ref)


def precond(sign, msg, mats):
    return pl.pallas_call(
        precond_kernel,
        out_shape=shape_of((N_DOM, 112, 128), BF16),
        in_specs=[SMEM_SPEC, VMEM_SPEC, HBM_SPEC],
        out_specs=VMEM_SPEC,
        scratch_shapes=[
            pltpu.VMEM((2, CASES, LOCAL), BF16),
            pltpu.VMEM((2, 3, LOCAL, 512), BF16),
            pltpu.SemaphoreType.DMA((2, 3)),
        ],
        compiler_params=params(52),
        name="precond",
    )(sign, msg, mats)


def tile_sums(msg_ref):
    total = jnp.zeros((16, 128), F32)
    for j in range(N_DOM):
        total += msg_ref[j].astype(F32)
    return total[:8] + total[8:]


def rho_kernel(msg_ref, ids_ref, out_ref):
    tile = tile_sums(msg_ref)
    for b in range(N_BLK):
        out_ref[b, pl.ds(0, 8), :] = tile
        out_ref[b, pl.ds(8, 8), :] = ids_ref[b]


def rho_parts(msg, ids):
    return pl.pallas_call(
        rho_kernel,
        grid=(1,),
        out_shape=shape_of((N_BLK, 16, 128), F32),
        in_specs=[pl.BlockSpec((N_DOM, 16, 128), lambda i: (0, 6, 0)), whole((N_BLK, 8, 128))],
        out_specs=whole((N_BLK, 16, 128)),
        compiler_params=params(),
        name="rho_parts",
    )(msg, ids)


def faces_kernel(place_ref, msg_ref, out_ref, both_ref):
    scatter_slots(msg_ref, place_ref, both_ref)
    out_ref[...] = both_ref[:COL_FACES] + both_ref[COL_FACES:]


def face_sums(place, msg):
    return pl.pallas_call(
        faces_kernel,
        out_shape=shape_of((COL_FACES, 8, 128), F32),
        in_specs=[SMEM_SPEC, VMEM_SPEC],
        out_specs=VMEM_SPEC,
        scratch_shapes=[pltpu.VMEM((COL_SLOTS, 8, 128), F32)],
        compiler_params=params(),
        name="face_sums",
    )(place, msg)


def all_of(parts_ref):
    return sum(parts_ref[b, pl.ds(0, 8), :] for b in range(N_BLK))


def direction_kernel(ids_ref, sign_ref, parts_ref, prev_ref, p_ref, msg_ref, out_ref, rho_ref, wide_ref):
    rho = jnp.sum(all_of(parts_ref), axis=1, keepdims=True) * (1.0 / TOTAL)
    rho_ref[...] = jnp.broadcast_to(rho, (8, 128))
    beta = jnp.broadcast_to(rho / prev_ref[:, :1], (8, 128))
    faces_wide(msg_ref, 48, wide_ref)
    wide_ref[...] = p_ref[...] + beta[None] * wide_ref[...]
    emit_slots(wide_ref, ids_ref, sign_ref, out_ref)


def directions(ids, sign, parts, prev, p, msg):
    return pl.pallas_call(
        direction_kernel,
        out_shape=(shape_of((N_DOM, 96, 128), BF16), shape_of((8, 128), F32)),
        in_specs=[SMEM_SPEC, SMEM_SPEC] + [VMEM_SPEC] * 4,
        out_specs=(VMEM_SPEC, VMEM_SPEC),
        scratch_shapes=[pltpu.VMEM((COL_FACES, 8, 128), F32)],
        compiler_params=params(),
        name="directions",
    )(ids, sign, parts, prev, p, msg)


def corner_kernel(msg_ref, coupling_ref, x_hbm, out_ref, x_ref, sem):
    unpack_slots(msg_ref, x_ref)
    store = pltpu.make_async_copy(x_ref, x_hbm, sem.at[0])
    store.start()
    for s in range(2):
        terms = lax.dot_general(
            coupling_ref[s], x_ref[s], (((1,), (1,)), ((), ())), preferred_element_type=F32
        )
        for b in range(N_BLK):
            out_ref[b, :, pl.ds(64 * s, 64)] = terms[32 * b : 32 * b + 32].astype(BF16)
    store.wait()


def corners(msg, coupling):
    return pl.pallas_call(
        corner_kernel,
        out_shape=(shape_of((2, CASES, LOCAL), BF16), shape_of((N_BLK, 32, 128), BF16)),
        in_specs=[VMEM_SPEC, VMEM_SPEC],
        out_specs=(HBM_SPEC, VMEM_SPEC),
        scratch_shapes=[pltpu.VMEM((2, CASES, LOCAL), BF16), pltpu.SemaphoreType.DMA((1,))],
        compiler_params=params(),
        name="corners",
    )(msg, coupling)


def dual_kernel(x_hbm, mat_hbm, out_ref, sum_ref, x_ref, mat_ref, x_sem, sems):
    load = pltpu.make_async_copy(x_hbm, x_ref, x_sem.at[0])
    load.start()
    copies = [load_columns(mat_hbm.at[s], mat_ref.at[s], sems.at[s]) for s in range(2)]
    load.wait()
    acc = jnp.zeros((CASES, 128), F32)
    for s in range(2):
        for q in range(3):
            copies[s][q].wait()
            lanes = pl.ds(512 * q, 512)
            y = jnp.dot(x_ref[s], mat_ref[s, q], preferred_element_type=F32)
            out_ref[s, :, lanes] = y
            acc += lane_tiles(x_ref[s, :, lanes].astype(F32) * y)
    sum_ref[...] = acc


def dual(x, mats):
    return pl.pallas_call(
        dual_kernel,
        out_shape=(shape_of((2, CASES, LOCAL), F32), shape_of((CASES, 128), F32)),
        in_specs=[HBM_SPEC, HBM_SPEC],
        out_specs=(VMEM_SPEC, VMEM_SPEC),
        scratch_shapes=[
            pltpu.VMEM((2, CASES, LOCAL), BF16),
            pltpu.VMEM((2, 3, LOCAL, 512), BF16),
            pltpu.SemaphoreType.DMA((1,)),
            pltpu.SemaphoreType.DMA((2, 3)),
        ],
        compiler_params=params(52),
        cost_estimate=pl.CostEstimate(
            flops=4 * CASES * LOCAL * LOCAL, bytes_accessed=4 * LOCAL * LOCAL, transcendentals=0
        ),
        name="dual",
    )(x, mats)


def matrix_kernel(parts_ref, after_ref, inv_ref, out_ref, hot_ref):
    lane = lax.broadcasted_iota(jnp.int32, (1, 128), 1) // 32
    spot = lax.broadcasted_iota(jnp.int32, (CB, 128), 0)
    for group in range(4):
        s, half = divmod(group, 2)
        ids = parts_ref[4 * half, pl.ds(8 + s, 1), :]
        for i in range(1, 4):
            ids = jnp.where(lane == i, parts_ref[4 * half + i, pl.ds(8 + s, 1), :], ids)
        hot = spot == jnp.broadcast_to(ids.astype(jnp.int32), (CB, 128))
        hot_ref[:, pl.ds(128 * group, 128)] = hot.astype(F32).astype(BF16)
    hot = hot_ref[...]
    columns = jnp.dot(inv_ref[...], hot, preferred_element_type=F32).astype(BF16)
    picked = lax.dot_general(hot, columns, (((0,), (0,)), ((), ())), preferred_element_type=F32)
    out_ref[...] = picked.astype(BF16)


def corner_matrix(parts, after, inv):
    return pl.pallas_call(
        matrix_kernel,
        out_shape=shape_of((512, 512), BF16),
        in_specs=[VMEM_SPEC, HBM_SPEC, VMEM_SPEC],
        out_specs=VMEM_SPEC,
        scratch_shapes=[pltpu.VMEM((CB, 512), BF16)],
        compiler_params=params(),
        cost_estimate=pl.CostEstimate(
            flops=2 * CB * 512 * (CB + 512), bytes_accessed=4 * CB * CB, transcendentals=0
        ),
        name="corner_matrix",
    )(parts, after, inv)


def lane_of(index):
    return lax.broadcasted_iota(jnp.int32, (8, 128), 1) == index


def packed(columns, base):
    stats = jnp.zeros((8, 128), F32)
    for k, value in enumerate(columns):
        high, rest = split_two(jnp.broadcast_to(value, (8, 128)))
        stats = jnp.where(lane_of(base + k), high, stats)
        stats = jnp.where(lane_of(base + 64 + k), rest, stats)
    high, rest = split_two(stats)
    return pair(high, rest).astype(BF16)


def solve_kernel(matrix_ref, terms_ref, sum_ref, out_ref, rhs_ref):
    terms = terms_ref[...].reshape(256, 128)
    rhs_ref[pl.ds(0, 256), :] = terms[:, :64]
    rhs_ref[pl.ds(256, 256), :] = terms[:, 64:]
    got = jnp.dot(matrix_ref[...], rhs_ref[...], preferred_element_type=F32).astype(BF16)
    for b in range(N_BLK):
        out_ref[b, pl.ds(0, 32), pl.ds(0, 64)] = got[32 * b : 32 * b + 32]
        out_ref[b, pl.ds(0, 32), pl.ds(64, 64)] = got[256 + 32 * b : 288 + 32 * b]
    coarse = jnp.sum(rhs_ref[...].astype(F32) * got.astype(F32), axis=0, keepdims=True)
    coarse = jnp.broadcast_to(coarse, (8, CASES))
    at_row = lax.broadcasted_iota(jnp.int32, (8, CASES), 0)
    at_lane = lax.broadcasted_iota(jnp.int32, (8, CASES), 1)
    columns = []
    for g in range(8):
        rows = pl.ds(8 * g, 8)
        value = jnp.sum(sum_ref[rows, :], axis=1, keepdims=True)
        spread = jnp.where(at_lane == at_row + 8 * g, coarse, 0.0)
        columns.append(value + jnp.sum(spread, axis=1, keepdims=True))
    tile = packed(columns, 0)
    for b in range(N_BLK):
        out_ref[b, pl.ds(32, 16), :] = tile


def solve(matrix, terms, sums):
    return pl.pallas_call(
        solve_kernel,
        out_shape=shape_of((N_BLK, 48, 128), BF16),
        in_specs=[VMEM_SPEC] * 3,
        out_specs=VMEM_SPEC,
        scratch_shapes=[pltpu.VMEM((512, CASES), BF16)],
        compiler_params=params(),
        name="solve",
    )(matrix, terms, sums)


def image_kernel(sign_ref, picks_ref, dual_ref, coupling_ref, out_ref):
    picks = picks_ref[:, pl.ds(0, 32), :].reshape(NCD, 128)
    for s in range(2):
        coarse = lax.dot_general(
            picks[:, 64 * s : 64 * s + 64],
            coupling_ref[s],
            (((0,), (0,)), ((), ())),
            preferred_element_type=F32,
        )
        for q in range(3):
            lanes = slice(512 * q, 512 * q + 512)
            y = dual_ref[s, :, lanes] + coarse[:, lanes]
            send_rows(y, s, q, sign_ref, out_ref)
    total = jnp.zeros((16, 128), F32)
    for b in range(N_BLK):
        total += picks_ref[b, pl.ds(32, 16), :].astype(F32)
    high, low = split_two(total[:8] + total[8:])
    tile = pair(high, low).astype(BF16)
    for i in range(N_DOM):
        out_ref[i, pl.ds(96, 16), :] = tile


def image_rows(sign, picks, dual_y, coupling):
    return pl.pallas_call(
        image_kernel,
        out_shape=shape_of((N_DOM, 112, 128), BF16),
        in_specs=[SMEM_SPEC] + [VMEM_SPEC] * 3,
        out_specs=VMEM_SPEC,
        compiler_params=params(),
        name="image_rows",
    )(sign, picks, dual_y, coupling)


def back_kernel(place_ref, at_ref, msg_ref, p_ref, first_ref, rho_ref, out_ref, both_ref):
    scatter_slots(msg_ref, place_ref, both_ref)
    total = jnp.zeros((16, 128), F32)
    for j in range(N_DOM):
        total += msg_ref[j, pl.ds(96, 16), :].astype(F32)
    base = at_ref[0]
    half = (1 - at_ref[1]).astype(F32)
    both = total[:8] + total[8:]
    lane8 = lax.broadcasted_iota(jnp.int32, (8, CASES), 1) * 8
    mine = jnp.where(lane8 == base, both[:, :64] + both[:, 64:], 0.0)
    curve = jnp.sum(mine, axis=1, keepdims=True) * (1.0 / TOTAL)
    rho = rho_ref[:, :1]
    alpha = rho / curve
    wide = jnp.broadcast_to(alpha, (8, 128))
    s0 = jnp.zeros((8, 128), F32)
    s2 = jnp.zeros((8, 128), F32)
    for o in range(N_DOM):
        for q in range(FACES // 2):
            f = FACES * o + 2 * q
            one = both_ref[f] + both_ref[COL_FACES + f]
            two = both_ref[f + 1] + both_ref[COL_FACES + f + 1]
            res = first_ref[o, pl.ds(16 * q, 16), :].astype(F32)
            new_one = res[:8] - wide * one
            new_two = res[8:] - wide * two
            s0 += res[:8] * res[:8] + res[8:] * res[8:]
            s2 += new_one * new_one + new_two * new_two
            out_ref[o, pl.ds(16 * q, 16), :] = pair(one, two).astype(BF16)
            out_ref[o, pl.ds(48 + 16 * q, 16), :] = pair(p_ref[f], p_ref[f + 1]).astype(BF16)
    sums = (
        rho * half,
        alpha * half,
        jnp.sum(s0, axis=1, keepdims=True),
        jnp.sum(s2, axis=1, keepdims=True),
    )
    tile = packed(sums, base)
    for o in range(N_DOM):
        out_ref[o, pl.ds(96, 16), :] = tile


def back(place, at, msg, p, first, rho):
    return pl.pallas_call(
        back_kernel,
        out_shape=shape_of((N_DOM, 112, 128), BF16),
        in_specs=[SMEM_SPEC, SMEM_SPEC] + [VMEM_SPEC] * 4,
        out_specs=VMEM_SPEC,
        scratch_shapes=[pltpu.VMEM((COL_SLOTS, 8, 128), F32)],
        compiler_params=params(),
        name="back",
    )(place, at, msg, p, first, rho)


def sums_kernel(msg_ref, out_ref):
    tile = tile_sums(msg_ref)
    for b in range(N_BLK):
        out_ref[b] = tile


def sums_parts(msg):
    return pl.pallas_call(
        sums_kernel,
        grid=(1,),
        out_shape=shape_of((N_BLK, 8, 128), F32),
        in_specs=[pl.BlockSpec((N_DOM, 16, 128), lambda i: (0, 6, 0))],
        out_specs=whole((N_BLK, 8, 128)),
        compiler_params=params(),
        name="sums_parts",
    )(msg)


def in_a_row(column):
    at_row = lax.broadcasted_iota(jnp.int32, (8, CASES), 0)
    at_lane = lax.broadcasted_iota(jnp.int32, (8, CASES), 1)
    row = jnp.zeros((1, CASES), F32)
    for g, value in enumerate(column):
        spread = jnp.where(at_lane == at_row + 8 * g, jnp.broadcast_to(value, (8, CASES)), 0.0)
        row += jnp.sum(spread, axis=0, keepdims=True)
    return row


def final_kernel(stats_ref, prev_ref, msg_ref, lam_ref, res_ref, dir_ref, lam_out, res_out, dir_out, rho_out):
    total = stats_ref[0, :, :64] + stats_ref[0, :, 64:]
    rho_now = []
    for g in range(8):
        rho = total[:, 8 * g : 8 * g + 1]
        rho_now.append(rho)
        rows = pl.ds(8 * g, 8)
        alpha = jnp.broadcast_to(total[:, 8 * g + 1 : 8 * g + 2], (8, 128))
        beta = jnp.broadcast_to(rho / prev_ref[rows, :], (8, 128))
        for h in range(2):
            lanes = pl.ds(128 * h, 128)
            for q in range(FACES // 2):
                image = msg_ref[2 * g + h, pl.ds(16 * q, 16), :].astype(F32)
                p = msg_ref[2 * g + h, pl.ds(48 + 16 * q, 16), :].astype(F32)
                for k in range(2):
                    f = 2 * q + k
                    half = slice(8 * k, 8 * k + 8)
                    direction = p[half] + beta * dir_ref[f, rows, lanes]
                    dir_out[f, rows, lanes] = direction
                    lam_out[f, rows, lanes] = lam_ref[f, rows, lanes] + alpha * direction
                    res_out[f, rows, lanes] = res_ref[f, rows, lanes] - alpha * image[half]
    rho_out[...] = in_a_row(rho_now)


def final(stats, prev, msg, lam, res, dirp):
    field = shape_of((FACES, CASES, FDOF), F32)
    return pl.pallas_call(
        final_kernel,
        out_shape=(field, field, field, shape_of((1, CASES), F32)),
        in_specs=[VMEM_SPEC] * 6,
        out_specs=(VMEM_SPEC,) * 4,
        compiler_params=params(),
        cost_estimate=pl.CostEstimate(
            flops=8 * FACES * CASES * FDOF, bytes_accessed=28 * FACES * CASES * FDOF, transcendentals=0
        ),
        name="final",
    )(stats, prev, msg, lam, res, dirp)


def reduction_kernel(parts_ref, out_ref):
    both = all_of(parts_ref)
    total = both[:, :64] + both[:, 64:]
    columns = [
        total[:, 8 * g + 3 : 8 * g + 4] / total[:, 8 * g + 2 : 8 * g + 3] for g in range(8)
    ]
    out_ref[...] = in_a_row(columns)


def reductions(parts):
    return pl.pallas_call(
        reduction_kernel,
        out_shape=shape_of((1, CASES), F32),
        in_specs=[VMEM_SPEC],
        out_specs=VMEM_SPEC,
        compiler_params=params(),
        name="reductions",
    )(parts)


def exchange(value, axis):
    return lax.all_to_all(value, axis, 0, 0, tiled=True)


def on_device(
    multipliers,
    residual,
    dir_prev,
    rho_prev,
    face_ids,
    face_sign,
    dual_blocks,
    dirichlet_blocks,
    coupling,
    corner_ids,
    coarse_inv,
):
    me = lax.axis_index(DOM)
    case_group = me // 2
    ids = face_ids[0].reshape(-1)
    sign_int = face_sign[0].reshape(-1)
    sign = sign_int.astype(F32)
    place = jnp.where(sign_int < 0, ids + COL_FACES, ids)
    my_sign = lax.dynamic_slice_in_dim(sign, me * SLOTS, SLOTS)
    at = jnp.stack([8 * case_group, me % 2]).astype(jnp.int32)
    block_ids = jnp.swapaxes(corner_ids[0].reshape(2, N_BLK, 32), 0, 1) - CB * jnp.arange(N_BLK)[:, None, None]
    block_ids = jnp.tile(block_ids.astype(F32), (1, 4, 4))
    prev = rho_prev[:, None]
    prev_mine = jnp.broadcast_to(lax.dynamic_slice_in_dim(prev, 8 * case_group, 8), (8, 128))

    first = exchange(pack(residual[0], dir_prev[0]), DOM)
    slots = exchange(pull(ids, sign, first), DOM)
    rows = exchange(precond(my_sign, slots, dirichlet_blocks[0]), DOM)
    parts = exchange(rho_parts(rows, block_ids), BLK)
    p = face_sums(place, rows)
    out_slots, rho = directions(ids, sign, parts, prev_mine, p, first)
    dir_slots = exchange(out_slots, DOM)
    matrix = corner_matrix(parts, rho, coarse_inv[0, 0])
    dir_slots, matrix = lax.optimization_barrier((dir_slots, matrix))
    x, terms = corners(dir_slots, coupling[0])
    dual_y, dual_sums = dual(x, dual_blocks[0])
    terms = exchange(terms, BLK)
    picks = exchange(solve(matrix, terms, dual_sums), BLK)
    image = exchange(image_rows(my_sign, picks, dual_y, coupling[0]), DOM)
    msg = exchange(back(place, at, image, p, first, rho), DOM)
    stats = sums_parts(msg)
    lam, res, direction, rho_now = final(stats, prev, msg, multipliers[0], residual[0], dir_prev[0])
    reduction = reductions(exchange(stats, BLK))
    return (lam[None], res[None], direction[None], rho_now[0], reduction[0])


def solution(mesh):
    split = Mesh(mesh.devices.reshape(4, 4, 4, 2), ("dom_0", "dom_1", "blk_0", "blk_1"))
    in_specs = (
        P(BLK, DOM, None, None),
        P(BLK, DOM, None, None),
        P(BLK, DOM, None, None),
        P(),
        P(BLK, None, None),
        P(BLK, None, None),
        P(BLK, DOM, None, None),
        P(BLK, DOM, None, None),
        P(BLK, DOM, None, None),
        P(BLK, DOM, None),
        P(DOM, BLK, None, None),
    )
    out_specs = (
        P(BLK, DOM, None, None),
        P(BLK, DOM, None, None),
        P(BLK, DOM, None, None),
        P(),
        P(),
    )
    return jax.shard_map(
        on_device, mesh=split, in_specs=in_specs, out_specs=out_specs, check_vma=False
    )
```
